256 devices in a mesh: ctx: 128 (over x, y, z), tp: 2 (over core).
Axes of the slice: x: 4, y: 4, z: 8, core: 2. Of those that a mesh axis runs over, the one named last changes fastest.
Arguments:
- x_in: bfloat16 [16384, 32, 128], P('ctx', 'tp'), may hold values from -60 to 60
- z_in: bfloat16 [16384, 32, 128], P('ctx', 'tp'), may hold values from -6 to 6
- b_in: bfloat16 [16384, 128], P('ctx'), may hold values from -0.29882812 to 0.29882812
- c_in: bfloat16 [16384, 128], P('ctx'), may hold values from -0.5 to 0.5
- log_decay: float32 [32, 16384], P('tp', 'ctx'), may hold values from -1 to 0
- d_skip: float32 [32], P('tp'), may hold values from 0.5 to 1.5
- norm_gain: float32 [32, 128], P('tp'), may hold values from 0.1 to 1.9
- w_out: bfloat16 [4096, 2048], P('tp'), may hold values from -0.09375 to 0.09375
Outputs:
- mixed: bfloat16 [16384, 2048], P(('ctx', 'tp'))
The draws below stay inside these ranges and needn't reach their ends.
All inputs are finite; a program needn't handle non-finite values.
Results may differ from the reference program's by a relative error of at most 0.005.
Values sent between devices are 32-bit elements; how exact they have to be, the bound alone decides.
No kernel may reach another device: no remote copies, remote signals or barrier semaphores. Data moves between devices by JAX's collectives and lax.ppermute only.
A program may use at most 320 MiB of HBM per device.

```python
import math
import jax
import jax.numpy as jnp
from jax import lax

D = 2048
ATTENTION_GROUPS = 32
P_SIZE = 128
N = 128
TOK_DEV = 128
TOKENS = 16384


def draw_x_in(key, part):
    key = jax.random.fold_in(key, 23)
    sampler_seeds = jax.random.split(key, 3)
    base = jax.random.normal(sampler_seeds[0], (TOKENS, ATTENTION_GROUPS, P_SIZE), jnp.float32)
    rows = jnp.exp(jax.random.uniform(sampler_seeds[1], (TOKENS, 1, 1), jnp.float32, 0.0, math.log(10.0)))
    columns = jnp.exp(jax.random.uniform(sampler_seeds[2], (1, ATTENTION_GROUPS, P_SIZE), jnp.float32, 0.0, math.log(10.0)))
    payload_vectors = base * rows * columns / 3.0
    return jnp.clip(payload_vectors, -60.0, 60.0).astype(jnp.bfloat16)


def draw_log_decay(key, part):
    key = jax.random.fold_in(key, 11)
    sampler_seeds = jax.random.split(key, 7)
    slow_share = 0.5
    slow = jax.random.bernoulli(sampler_seeds[0], slow_share, (ATTENTION_GROUPS, 1))
    fast_rate = 1.0 / jax.random.uniform(sampler_seeds[1], (ATTENTION_GROUPS, 1), jnp.float32, 30.0, 50.0)
    slow_rate = jax.random.uniform(sampler_seeds[2], (ATTENTION_GROUPS, 1), jnp.float32, 0.3, 0.6) / TOKENS
    forgetting_factor = jnp.where(slow, slow_rate, fast_rate)
    approximate_guess = jax.random.uniform(sampler_seeds[3], (ATTENTION_GROUPS, TOKENS), jnp.float32, 0.5, 1.5)
    processor_number = jnp.exp(jax.random.uniform(sampler_seeds[4], (ATTENTION_GROUPS, TOKENS // TOK_DEV), jnp.float32, -0.35, 0.35))
    processor_number = jnp.repeat(processor_number, TOK_DEV, axis=1)
    spots = jax.random.randint(sampler_seeds[5], (2,), 0, TOKENS)
    match_tally = jnp.sum((jnp.arange(TOKENS)[None, :] == spots[:, None]).astype(jnp.float32), axis=0)
    segment_span = jax.random.uniform(sampler_seeds[6], (ATTENTION_GROUPS, 1), jnp.float32, 0.22, 0.69)
    payload_vectors = -(forgetting_factor * approximate_guess * processor_number) - segment_span * match_tally[None, :]
    return jnp.clip(payload_vectors, -1.0, 0.0).astype(jnp.float32)


def shard_levels(key, shape, cuts, least, largest):
    gain = 1.0
    for position, parts in cuts:
        draws = jax.random.uniform(jax.random.fold_in(jax.random.fold_in(key, 6), position), (parts,), jnp.float32, least / len(cuts), largest / len(cuts))
        gain = gain * jnp.repeat(jnp.exp(draws), shape[position] // parts).reshape((-1,) + (1,) * (len(shape) - 1 - position))
    return gain


def noise(own_key, shape, spread, reach, cuts=(), kind=jnp.bfloat16):
    array = jax.random.normal(own_key, shape, jnp.float32) * spread
    if len(cuts) > 0:
        array = shard_levels(own_key, shape, cuts, -0.22, 0.18) * array
    return jnp.clip(array, min=-reach, max=reach).astype(kind)


def setup_inputs(seed: int = 0) -> dict:
    key_of = jax.random.split(jax.random.key(seed), 9)
    x_in = draw_x_in(jax.random.fold_in(key_of[8], 71), 0)
    z_in = noise(key_of[1], (TOKENS, ATTENTION_GROUPS, P_SIZE), 1.0, 6.0, ((0, 128), (1, 2)))
    b_in = noise(key_of[2], (TOKENS, N), 0.05, 0.29882812, ((0, 128),))
    c_in = noise(key_of[3], (TOKENS, N), N ** -0.5, 0.5, ((0, 128),))
    log_decay = draw_log_decay(jax.random.fold_in(key_of[8], 71), 0)
    d_skip = jnp.clip(0.5 + 1.0 * jax.random.uniform(key_of[5], (ATTENTION_GROUPS,), jnp.float32) ** shard_levels(key_of[5], (ATTENTION_GROUPS,), ((0, 2),), -0.2, 0.2), 0.5, 1.5)
    norm_gain = jnp.clip(1.0 + 0.18 * jax.random.normal(key_of[6], (ATTENTION_GROUPS, P_SIZE), jnp.float32), 0.1, 1.9)
    w_out = noise(key_of[7], (ATTENTION_GROUPS * P_SIZE, D), (ATTENTION_GROUPS * P_SIZE) ** -0.5, 0.09375, ((0, 2),))
    return dict(x_in=x_in, z_in=z_in, b_in=b_in, c_in=c_in, log_decay=log_decay, d_skip=d_skip, norm_gain=norm_gain, w_out=w_out)


def reference(x_in, z_in, b_in, c_in, log_decay, d_skip, norm_gain, w_out):
    block = min(128, TOK_DEV)
    count = TOKENS // block
    highest = lax.Precision.HIGHEST
    xs = x_in.reshape(count, block, ATTENTION_GROUPS, P_SIZE)
    zs = z_in.reshape(count, block, ATTENTION_GROUPS, P_SIZE)
    bs = b_in.reshape(count, block, N)
    cs = c_in.reshape(count, block, N)
    decays = log_decay.reshape(ATTENTION_GROUPS, count, block).transpose(1, 0, 2)
    positions = jnp.arange(block)
    lower = positions[:, None] >= positions[None, :]

    def advance(state, pieces):
        x_blk, z_blk, b_blk, c_blk, decay_blk = pieces
        cum = jnp.cumsum(decay_blk, axis=1)
        differ = cum[:, :, None] - cum[:, None, :]
        within = jnp.where(lower[None], jnp.exp(jnp.where(lower[None], differ, 0.0)), 0.0)
        scores = jnp.dot(c_blk, b_blk.T, preferred_element_type=jnp.float32)
        block_weights = (within * scores[None]).astype(jnp.bfloat16)
        x_wide = x_blk.astype(jnp.float32)
        b_wide = b_blk.astype(jnp.float32)
        c_wide = c_blk.astype(jnp.float32)
        inner = jnp.einsum('hts,shp->thp', block_weights.astype(jnp.float32), x_wide, precision=highest)
        carried = jnp.einsum('tn,hnp->thp', c_wide, state, precision=highest)
        carried = jnp.exp(cum).T[:, :, None] * carried
        ssm_out = inner + carried + d_skip[None, :, None] * x_wide
        last = cum[:, -1]
        weights = jnp.exp(last[:, None] - cum)
        fresh = jnp.einsum('sn,shp->hnp', b_wide, x_wide * weights.T[:, :, None], precision=highest)
        new_state = jnp.exp(last)[:, None, None] * state + fresh
        gated = ssm_out * jax.nn.silu(z_blk.astype(jnp.float32))
        meansq = lax.optimization_barrier(jnp.mean(gated * gated, axis=-1, keepdims=True))
        normed = (gated * lax.rsqrt(meansq + 1e-05) * norm_gain[None]).astype(jnp.bfloat16)
        result = jnp.dot(normed.reshape(block, ATTENTION_GROUPS * P_SIZE), w_out, preferred_element_type=jnp.float32)
        return (new_state, result.astype(jnp.bfloat16))
    start = jnp.zeros((ATTENTION_GROUPS, N, P_SIZE), jnp.float32)
    _, outputs = lax.scan(advance, start, (xs, zs, bs, cs, decays))
    return outputs.reshape(TOKENS, D)
```

```python
import functools

import jax
import jax.numpy as jnp
from jax import lax
from jax.experimental import pallas as pl
from jax.experimental.pallas import tpu as pltpu
from jax.sharding import PartitionSpec as P

F32 = jnp.float32
BF16 = jnp.bfloat16
HIGHEST = lax.Precision.HIGHEST
NX, NY, NZ = 4, 4, 8
HEADS = 16
W = 128
CHUNKS = 2
PER_CHUNK = HEADS // CHUNKS
OWN = PER_CHUNK // NZ
ROWS = OWN * W
MSG = ROWS + 8
VMEM = pl.BlockSpec(memory_space=pltpu.VMEM)
SMEM = pl.BlockSpec(memory_space=pltpu.SMEM)


def z_shift(k):
    return [(i, i // NZ * NZ + (i + k) % NZ) for i in range(NX * NY * NZ)]


def y_shift(k):
    span = NY * NZ
    return [(i, i // span * span + (i + k * NZ) % span) for i in range(NX * NY * NZ)]


def x_shift(k):
    total = NX * NY * NZ
    return [(i, (i + k * NY * NZ) % total) for i in range(total)]


def split(value):
    high = value.astype(BF16)
    return high, (value - high.astype(F32)).astype(BF16)


def lower_mask():
    rows = lax.broadcasted_iota(jnp.int32, (W, W), 0)
    columns = lax.broadcasted_iota(jnp.int32, (W, W), 1)
    return rows >= columns


def running_sum(log_decay):
    upper = jnp.where(lower_mask(), 1.0, 0.0).T
    return jnp.dot(log_decay, upper, precision=HIGHEST, preferred_element_type=F32)


def decay_tile(rows):
    place = lax.broadcasted_iota(jnp.int32, (8, W), 0)
    tile = jnp.zeros((8, W), F32)
    for i, row in enumerate(rows):
        tile = jnp.where(place == i, jnp.broadcast_to(row, (8, W)), tile)
    return tile


def local_state_kernel(chunk, pos, x, b, log_decay, *refs):
    outs, cum_ref = refs[:NZ], refs[NZ]
    cum_ref[...] = running_sum(log_decay[...])
    b_t = b[...].astype(F32).T
    for k in range(NZ):
        owner = (pos[0] + k) & (NZ - 1)
        lasts = []
        for i in range(OWN):
            head = chunk * PER_CHUNK + owner * OWN + i
            cum = cum_ref[pl.ds(head, 1), :]
            last = jnp.broadcast_to(cum[:, W - 1 :], (1, W))
            high, low = split(b_t * jnp.exp(last - cum))
            x_head = x[:, pl.ds(pl.multiple_of(head * W, W), W)]
            state = jnp.dot(high, x_head, preferred_element_type=F32)
            state += jnp.dot(low, x_head, preferred_element_type=F32)
            outs[k][i * W : (i + 1) * W, :] = state
            lasts.append(last)
        outs[k][ROWS:, :] = decay_tile(lasts)


def row_total_kernel(pos, *refs):
    parts, out = refs[:NZ], refs[NZ]
    places = [(pos[0] - k) & (NZ - 1) for k in range(NZ)]
    totals = []
    for i in range(OWN):
        logs = [part[ROWS + i : ROWS + i + 1, :] for part in parts]
        total = jnp.zeros((W, W), F32)
        for k in range(NZ):
            after = jnp.zeros((1, W), F32)
            for j in range(NZ):
                if j != k:
                    after += jnp.where(places[j] > places[k], logs[j], 0.0)
            total += jnp.exp(after) * parts[k][i * W : (i + 1) * W, :]
        out[i * W : (i + 1) * W, :] = total
        totals.append(sum(logs))
    out[ROWS:, :] = decay_tile(totals)


def plane_kernel(pos, *refs):
    parts, plane, before = refs[:NY], refs[NY], refs[NY + 1]
    places = [(pos[1] - k) & (NY - 1) for k in range(NY)]
    plane_logs, before_logs = [], []
    for i in range(OWN):
        logs = [part[ROWS + i : ROWS + i + 1, :] for part in parts]
        total = jnp.zeros((W, W), F32)
        earlier = jnp.zeros((W, W), F32)
        to_row = jnp.zeros((1, W), F32)
        for k in range(NY):
            after = jnp.zeros((1, W), F32)
            between = jnp.zeros((1, W), F32)
            for j in range(NY):
                if j != k:
                    later = jnp.where(places[j] > places[k], logs[j], 0.0)
                    after += later
                    between += jnp.where(places[j] < pos[1], later, 0.0)
            piece = parts[k][i * W : (i + 1) * W, :]
            total += jnp.exp(after) * piece
            if k > 0:
                mine = places[k] < pos[1]
                earlier += jnp.where(mine, jnp.exp(between), 0.0) * piece
                to_row += jnp.where(mine, logs[k], 0.0)
        plane[i * W : (i + 1) * W, :] = total
        before[i * W : (i + 1) * W, :] = earlier
        plane_logs.append(sum(logs))
        before_logs.append(to_row)
    plane[ROWS:, :] = decay_tile(plane_logs)
    before[ROWS:, :] = decay_tile(before_logs)


def entering_kernel(pos, *refs):
    planes, before = refs[: NX - 1], refs[NX - 1]
    parts = refs[NX : NX + NZ]
    outs = refs[NX + NZ : NX + 2 * NZ]
    ordered, entering = refs[NX + 2 * NZ :]
    for k in range(NZ):
        ordered[(pos[0] - k) & (NZ - 1)] = parts[k][...]
    for i in range(OWN):
        carry = jnp.zeros((W, W), F32)
        between = jnp.zeros((1, W), F32)
        for k in range(1, NX):
            earlier = k <= pos[2]
            piece = planes[k - 1][i * W : (i + 1) * W, :]
            carry += jnp.where(earlier, jnp.exp(between), 0.0) * piece
            between += jnp.where(earlier, planes[k - 1][ROWS + i : ROWS + i + 1, :], 0.0)
        carry = jnp.exp(before[ROWS + i : ROWS + i + 1, :]) * carry
        carry += before[i * W : (i + 1) * W, :]
        for place in range(NZ):
            entering[place, i * W : (i + 1) * W, :] = carry
            if place < NZ - 1:
                decay = jnp.exp(ordered[place, ROWS + i : ROWS + i + 1, :])
                carry = decay * carry + ordered[place, i * W : (i + 1) * W, :]
    for k in range(NZ):
        outs[k][...] = entering[(pos[0] + k) & (NZ - 1)]


def inside_kernel(skip, x, z, b, c, log_decay, fixed, slope):
    lower = lower_mask()
    logs = log_decay[...]
    cum = running_sum(logs)
    cum_t = lax.dot_general(
        jnp.where(lower, 1.0, 0.0), logs, (((1,), (1,)), ((), ())),
        precision=HIGHEST, preferred_element_type=F32,
    )
    scores = lax.dot_general(c[...], b[...], (((1,), (1,)), ((), ())), preferred_element_type=F32)
    for head in range(HEADS):
        at = slice(head * W, (head + 1) * W)
        column = cum_t[:, head : head + 1]
        differ = column - cum[head : head + 1, :]
        within = jnp.where(lower, jnp.exp(jnp.where(lower, differ, 0.0)), 0.0)
        x_head = x[:, at]
        inner = jnp.dot((within * scores).astype(BF16), x_head, preferred_element_type=F32)
        gate = z[:, at].astype(F32)
        gate = gate / (1.0 + jnp.exp(-gate))
        fixed[:, at] = (inner + skip[head] * x_head.astype(F32)) * gate
        slope[:, at] = jnp.exp(column) * gate


def head_norm_kernel(chunk, pos, *refs):
    states = refs[:NZ]
    c, fixed, slope, gain, normed = refs[NZ:]
    read = c[...]
    for k in range(NZ):
        owner = (pos[0] - k) & (NZ - 1)
        for i in range(OWN):
            local = owner * OWN + i
            head = chunk * PER_CHUNK + local
            high, low = split(states[k][i * W : (i + 1) * W, :])
            carried = jnp.dot(read, high, preferred_element_type=F32)
            carried += jnp.dot(read, low, preferred_element_type=F32)
            at = pl.ds(pl.multiple_of(head * W, W), W)
            gated = fixed[:, at] + slope[:, at] * carried
            meansq = jnp.mean(gated * gated, axis=-1, keepdims=True)
            value = gated * lax.rsqrt(meansq + 1e-05) * gain[pl.ds(head, 1), :]
            normed[:, pl.ds(pl.multiple_of(local * W, W), W)] = value.astype(BF16)


def call(kernel, outs, specs, scratch=(), flops=0, moved=0, name=None):
    return pl.pallas_call(
        kernel,
        out_shape=outs,
        in_specs=specs,
        out_specs=jax.tree.map(lambda _: VMEM, outs),
        scratch_shapes=scratch,
        compiler_params=pltpu.CompilerParams(vmem_limit_bytes=24 * 1024 * 1024),
        cost_estimate=pl.CostEstimate(flops=flops, bytes_accessed=moved, transcendentals=0),
        name=name,
    )


def shaped(*shape, dtype=F32):
    return jax.ShapeDtypeStruct(shape, dtype)


def per_device(x_in, z_in, b_in, c_in, log_decay, d_skip, norm_gain, w_out):
    index = lax.axis_index("ctx")
    pos = jnp.stack([index % NZ, index // NZ % NY, index // (NZ * NY)]).astype(jnp.int32)
    x = x_in.reshape(W, HEADS * W)
    message = [shaped(MSG, W)] * NZ
    kept, normed_parts = {}, []
    for chunk in range(CHUNKS):
        kept[chunk] = call(
            functools.partial(local_state_kernel, chunk), message, [SMEM, VMEM, VMEM, VMEM],
            [pltpu.VMEM((HEADS, W), F32)], moved=1 << 20, name=f"local_state_{chunk}",
        )(pos, x, b_in, log_decay)
    z = z_in.reshape(W, HEADS * W)
    fixed, slope = call(
        inside_kernel, [shaped(W, HEADS * W)] * 2, [SMEM] + [VMEM] * 5, moved=8 << 20, name="inside",
    )(d_skip, x, z, b_in, c_in, log_decay)
    for chunk in range(CHUNKS):
        out = kept[chunk]
        parts = [out[0]] + [lax.ppermute(out[k], "ctx", z_shift(k)) for k in range(1, NZ)]
        total = call(row_total_kernel, shaped(MSG, W), [SMEM] + [VMEM] * NZ, name=f"row_total_{chunk}")(pos, *parts)
        rows = [total] + [lax.ppermute(total, "ctx", y_shift(k)) for k in range(1, NY)]
        plane, before = call(
            plane_kernel, [shaped(MSG, W)] * 2, [SMEM] + [VMEM] * NY, name=f"plane_{chunk}"
        )(pos, *rows)
        planes = [lax.ppermute(plane, "ctx", x_shift(k)) for k in range(1, NX)]
        back = call(
            entering_kernel, [shaped(ROWS, W)] * NZ, [SMEM] + [VMEM] * (NX + NZ),
            [pltpu.VMEM((NZ, MSG, W), F32), pltpu.VMEM((NZ, ROWS, W), F32)], name=f"entering_{chunk}",
        )(pos, *planes, before, *parts)
        states = [back[0]] + [lax.ppermute(back[k], "ctx", z_shift(k)) for k in range(1, NZ)]
        normed_parts.append(call(
            functools.partial(head_norm_kernel, chunk), shaped(W, PER_CHUNK * W, dtype=BF16),
            [SMEM] + [VMEM] * (NZ + 4), name=f"head_norm_{chunk}",
        )(pos, *states, c_in, fixed, slope, norm_gain))
    mixed = sum(
        jnp.dot(
            normed, w_out[chunk * PER_CHUNK * W : (chunk + 1) * PER_CHUNK * W],
            preferred_element_type=F32,
        )
        for chunk, normed in enumerate(normed_parts)
    )
    core = lax.axis_index("tp")
    half = W // 2
    mine = lax.dynamic_slice_in_dim(mixed, core * half, half, 0)
    other = lax.dynamic_slice_in_dim(mixed, (1 - core) * half, half, 0)
    return (mine + lax.ppermute(other, "tp", [(0, 1), (1, 0)])).astype(BF16)


def solution(mesh):
    return jax.shard_map(
        per_device,
        mesh=mesh,
        in_specs=(
            P("ctx", "tp", None),
            P("ctx", "tp", None),
            P("ctx", None),
            P("ctx", None),
            P("tp", "ctx"),
            P("tp"),
            P("tp", None),
            P("tp", None),
        ),
        out_specs=P(("ctx", "tp"), None),
        check_vma=False,
    )
```

```python
import functools

import jax
import jax.numpy as jnp
from jax import lax
from jax.experimental import pallas as pl
from jax.experimental.pallas import tpu as pltpu
from jax.sharding import PartitionSpec as P

F32 = jnp.float32
BF16 = jnp.bfloat16
HIGHEST = lax.Precision.HIGHEST
NX, NY, NZ = 4, 4, 8
HEADS = 16
W = 128
CHUNKS = 1
PER_CHUNK = HEADS // CHUNKS
OWN = PER_CHUNK // NZ
ROWS = OWN * W
MSG = ROWS + 8
VMEM = pl.BlockSpec(memory_space=pltpu.VMEM)
SMEM = pl.BlockSpec(memory_space=pltpu.SMEM)


def z_shift(k):
    return [(i, i // NZ * NZ + (i + k) % NZ) for i in range(NX * NY * NZ)]


def y_shift(k):
    span = NY * NZ
    return [(i, i // span * span + (i + k * NZ) % span) for i in range(NX * NY * NZ)]


def x_shift(k):
    total = NX * NY * NZ
    return [(i, (i + k * NY * NZ) % total) for i in range(total)]


def split(value):
    high = value.astype(BF16)
    return high, (value - high.astype(F32)).astype(BF16)


def lower_mask():
    rows = lax.broadcasted_iota(jnp.int32, (W, W), 0)
    columns = lax.broadcasted_iota(jnp.int32, (W, W), 1)
    return rows >= columns


def running_sum(log_decay):
    upper = jnp.where(lower_mask(), 1.0, 0.0).T
    return jnp.dot(log_decay, upper, precision=HIGHEST, preferred_element_type=F32)


def decay_tile(rows):
    place = lax.broadcasted_iota(jnp.int32, (8, W), 0)
    tile = jnp.zeros((8, W), F32)
    for i, row in enumerate(rows):
        tile = jnp.where(place == i, jnp.broadcast_to(row, (8, W)), tile)
    return tile


def local_state_kernel(chunk, pos, x, b, log_decay, *refs):
    outs, cum_ref = refs[:NZ], refs[NZ]
    cum_ref[...] = running_sum(log_decay[...])
    b_t = b[...].astype(F32).T
    for k in range(NZ):
        owner = (pos[0] + k) & (NZ - 1)
        lasts = []
        for i in range(OWN):
            head = chunk * PER_CHUNK + owner * OWN + i
            cum = cum_ref[pl.ds(head, 1), :]
            last = jnp.broadcast_to(cum[:, W - 1 :], (1, W))
            high, low = split(b_t * jnp.exp(last - cum))
            x_head = x[:, pl.ds(pl.multiple_of(head * W, W), W)]
            state = jnp.dot(high, x_head, preferred_element_type=F32)
            state += jnp.dot(low, x_head, preferred_element_type=F32)
            outs[k][i * W : (i + 1) * W, :] = state
            lasts.append(last)
        outs[k][ROWS:, :] = decay_tile(lasts)


def row_total_kernel(pos, *refs):
    parts, out = refs[:NZ], refs[NZ]
    places = [(pos[0] - k) & (NZ - 1) for k in range(NZ)]
    totals = []
    for i in range(OWN):
        logs = [part[ROWS + i : ROWS + i + 1, :] for part in parts]
        total = jnp.zeros((W, W), F32)
        for k in range(NZ):
            after = jnp.zeros((1, W), F32)
            for j in range(NZ):
                if j != k:
                    after += jnp.where(places[j] > places[k], logs[j], 0.0)
            total += jnp.exp(after) * parts[k][i * W : (i + 1) * W, :]
        out[i * W : (i + 1) * W, :] = total
        totals.append(sum(logs))
    out[ROWS:, :] = decay_tile(totals)


def plane_kernel(pos, *refs):
    parts, plane, before = refs[:NY], refs[NY], refs[NY + 1]
    places = [(pos[1] - k) & (NY - 1) for k in range(NY)]
    plane_logs, before_logs = [], []
    for i in range(OWN):
        logs = [part[ROWS + i : ROWS + i + 1, :] for part in parts]
        total = jnp.zeros((W, W), F32)
        earlier = jnp.zeros((W, W), F32)
        to_row = jnp.zeros((1, W), F32)
        for k in range(NY):
            after = jnp.zeros((1, W), F32)
            between = jnp.zeros((1, W), F32)
            for j in range(NY):
                if j != k:
                    later = jnp.where(places[j] > places[k], logs[j], 0.0)
                    after += later
                    between += jnp.where(places[j] < pos[1], later, 0.0)
            piece = parts[k][i * W : (i + 1) * W, :]
            total += jnp.exp(after) * piece
            if k > 0:
                mine = places[k] < pos[1]
                earlier += jnp.where(mine, jnp.exp(between), 0.0) * piece
                to_row += jnp.where(mine, logs[k], 0.0)
        plane[i * W : (i + 1) * W, :] = total
        before[i * W : (i + 1) * W, :] = earlier
        plane_logs.append(sum(logs))
        before_logs.append(to_row)
    plane[ROWS:, :] = decay_tile(plane_logs)
    before[ROWS:, :] = decay_tile(before_logs)


def entering_kernel(pos, *refs):
    planes, before = refs[: NX - 1], refs[NX - 1]
    parts = refs[NX : NX + NZ]
    outs = refs[NX + NZ : NX + 2 * NZ]
    ordered, entering = refs[NX + 2 * NZ :]
    for k in range(NZ):
        ordered[(pos[0] - k) & (NZ - 1)] = parts[k][...]
    for i in range(OWN):
        carry = jnp.zeros((W, W), F32)
        between = jnp.zeros((1, W), F32)
        for k in range(1, NX):
            earlier = k <= pos[2]
            piece = planes[k - 1][i * W : (i + 1) * W, :]
            carry += jnp.where(earlier, jnp.exp(between), 0.0) * piece
            between += jnp.where(earlier, planes[k - 1][ROWS + i : ROWS + i + 1, :], 0.0)
        carry = jnp.exp(before[ROWS + i : ROWS + i + 1, :]) * carry
        carry += before[i * W : (i + 1) * W, :]
        for place in range(NZ):
            entering[place, i * W : (i + 1) * W, :] = carry
            if place < NZ - 1:
                decay = jnp.exp(ordered[place, ROWS + i : ROWS + i + 1, :])
                carry = decay * carry + ordered[place, i * W : (i + 1) * W, :]
    for k in range(NZ):
        outs[k][...] = entering[(pos[0] + k) & (NZ - 1)]


def inside_kernel(skip, x, z, b, c, log_decay, fixed, slope):
    lower = lower_mask()
    logs = log_decay[...]
    cum = running_sum(logs)
    cum_t = lax.dot_general(
        jnp.where(lower, 1.0, 0.0), logs, (((1,), (1,)), ((), ())),
        precision=HIGHEST, preferred_element_type=F32,
    )
    scores = lax.dot_general(c[...], b[...], (((1,), (1,)), ((), ())), preferred_element_type=F32)
    for head in range(HEADS):
        at = slice(head * W, (head + 1) * W)
        column = cum_t[:, head : head + 1]
        differ = column - cum[head : head + 1, :]
        within = jnp.where(lower, jnp.exp(jnp.where(lower, differ, 0.0)), 0.0)
        x_head = x[:, at]
        inner = jnp.dot((within * scores).astype(BF16), x_head, preferred_element_type=F32)
        gate = z[:, at].astype(F32)
        gate = gate / (1.0 + jnp.exp(-gate))
        fixed[:, at] = (inner + skip[head] * x_head.astype(F32)) * gate
        slope[:, at] = jnp.exp(column) * gate


def head_norm_kernel(chunk, pos, *refs):
    states = refs[:NZ]
    c, fixed, slope, gain, normed = refs[NZ:]
    read = c[...]
    for k in range(NZ):
        owner = (pos[0] - k) & (NZ - 1)
        for i in range(OWN):
            local = owner * OWN + i
            head = chunk * PER_CHUNK + local
            high, low = split(states[k][i * W : (i + 1) * W, :])
            carried = jnp.dot(read, high, preferred_element_type=F32)
            carried += jnp.dot(read, low, preferred_element_type=F32)
            at = pl.ds(pl.multiple_of(head * W, W), W)
            gated = fixed[:, at] + slope[:, at] * carried
            meansq = jnp.mean(gated * gated, axis=-1, keepdims=True)
            value = gated * lax.rsqrt(meansq + 1e-05) * gain[pl.ds(head, 1), :]
            normed[:, pl.ds(pl.multiple_of(local * W, W), W)] = value.astype(BF16)


def call(kernel, outs, specs, scratch=(), flops=0, moved=0, name=None):
    return pl.pallas_call(
        kernel,
        out_shape=outs,
        in_specs=specs,
        out_specs=jax.tree.map(lambda _: VMEM, outs),
        scratch_shapes=scratch,
        compiler_params=pltpu.CompilerParams(vmem_limit_bytes=24 * 1024 * 1024),
        cost_estimate=pl.CostEstimate(flops=flops, bytes_accessed=moved, transcendentals=0),
        name=name,
    )


def shaped(*shape, dtype=F32):
    return jax.ShapeDtypeStruct(shape, dtype)


def per_device(x_in, z_in, b_in, c_in, log_decay, d_skip, norm_gain, w_out):
    index = lax.axis_index("ctx")
    pos = jnp.stack([index % NZ, index // NZ % NY, index // (NZ * NY)]).astype(jnp.int32)
    x = x_in.reshape(W, HEADS * W)
    message = [shaped(MSG, W)] * NZ
    kept, normed_parts = {}, []
    for chunk in range(CHUNKS):
        kept[chunk] = call(
            functools.partial(local_state_kernel, chunk), message, [SMEM, VMEM, VMEM, VMEM],
            [pltpu.VMEM((HEADS, W), F32)], moved=1 << 20, name=f"local_state_{chunk}",
        )(pos, x, b_in, log_decay)
    z = z_in.reshape(W, HEADS * W)
    fixed, slope = call(
        inside_kernel, [shaped(W, HEADS * W)] * 2, [SMEM] + [VMEM] * 5, moved=8 << 20, name="inside",
    )(d_skip, x, z, b_in, c_in, log_decay)
    for chunk in range(CHUNKS):
        out = kept[chunk]
        parts = [out[0]] + [lax.ppermute(out[k], "ctx", z_shift(k)) for k in range(1, NZ)]
        total = call(row_total_kernel, shaped(MSG, W), [SMEM] + [VMEM] * NZ, name=f"row_total_{chunk}")(pos, *parts)
        rows = [total] + [lax.ppermute(total, "ctx", y_shift(k)) for k in range(1, NY)]
        plane, before = call(
            plane_kernel, [shaped(MSG, W)] * 2, [SMEM] + [VMEM] * NY, name=f"plane_{chunk}"
        )(pos, *rows)
        planes = [lax.ppermute(plane, "ctx", x_shift(k)) for k in range(1, NX)]
        back = call(
            entering_kernel, [shaped(ROWS, W)] * NZ, [SMEM] + [VMEM] * (NX + NZ),
            [pltpu.VMEM((NZ, MSG, W), F32), pltpu.VMEM((NZ, ROWS, W), F32)], name=f"entering_{chunk}",
        )(pos, *planes, before, *parts)
        states = [back[0]] + [lax.ppermute(back[k], "ctx", z_shift(k)) for k in range(1, NZ)]
        normed_parts.append(call(
            functools.partial(head_norm_kernel, chunk), shaped(W, PER_CHUNK * W, dtype=BF16),
            [SMEM] + [VMEM] * (NZ + 4), name=f"head_norm_{chunk}",
        )(pos, *states, c_in, fixed, slope, norm_gain))
    mixed = sum(
        jnp.dot(
            normed, w_out[chunk * PER_CHUNK * W : (chunk + 1) * PER_CHUNK * W],
            preferred_element_type=F32,
        )
        for chunk, normed in enumerate(normed_parts)
    )
    core = lax.axis_index("tp")
    half = W // 2
    mine = lax.dynamic_slice_in_dim(mixed, core * half, half, 0)
    other = lax.dynamic_slice_in_dim(mixed, (1 - core) * half, half, 0)
    return (mine + lax.ppermute(other, "tp", [(0, 1), (1, 0)])).astype(BF16)


def solution(mesh):
    return jax.shard_map(
        per_device,
        mesh=mesh,
        in_specs=(
            P("ctx", "tp", None),
            P("ctx", "tp", None),
            P("ctx", None),
            P("ctx", None),
            P("tp", "ctx"),
            P("tp"),
            P("tp", None),
            P("tp", None),
        ),
        out_specs=P(("ctx", "tp"), None),
        check_vma=False,
    )
```

```python
import functools

import jax
import jax.numpy as jnp
from jax import lax
from jax.experimental import pallas as pl
from jax.experimental.pallas import tpu as pltpu
from jax.sharding import PartitionSpec as P

F32 = jnp.float32
BF16 = jnp.bfloat16
HIGHEST = lax.Precision.HIGHEST
NX, NY, NZ = 4, 4, 8
HEADS = 16
W = 128
CHUNKS = 1
PER_CHUNK = HEADS // CHUNKS
OWN = PER_CHUNK // NZ
ROWS = OWN * W
MSG = ROWS + 8
ORDER = (0, 1, 7, 2, 6, 3, 5, 4)
EARLY = 5
TILE = 512
HBM = pl.BlockSpec(memory_space=pltpu.HBM)
VMEM = pl.BlockSpec(memory_space=pltpu.VMEM)
SMEM = pl.BlockSpec(memory_space=pltpu.SMEM)


def z_shift(k):
    return [(i, i // NZ * NZ + (i + k) % NZ) for i in range(NX * NY * NZ)]


def partners(stride, k):
    return [(i, i ^ (stride * k)) for i in range(NX * NY * NZ)]


def split(value):
    high = value.astype(BF16)
    return high, (value - high.astype(F32)).astype(BF16)


def lower_mask():
    rows = lax.broadcasted_iota(jnp.int32, (W, W), 0)
    columns = lax.broadcasted_iota(jnp.int32, (W, W), 1)
    return rows >= columns


def running_sum(log_decay):
    upper = jnp.where(lower_mask(), 1.0, 0.0).T
    return jnp.dot(log_decay, upper, precision=HIGHEST, preferred_element_type=F32)


def decay_tile(rows):
    place = lax.broadcasted_iota(jnp.int32, (8, W), 0)
    tile = jnp.zeros((8, W), F32)
    for i, row in enumerate(rows):
        tile = jnp.where(place == i, jnp.broadcast_to(row, (8, W)), tile)
    return tile


def local_state_kernel(chunk, pos, x, b_hbm, log_decay_hbm, *refs):
    outs, (cum_ref, b, log_decay, sems) = refs[:NZ], refs[NZ:]
    copies = [
        pltpu.make_async_copy(log_decay_hbm, log_decay, sems.at[0]),
        pltpu.make_async_copy(b_hbm, b, sems.at[1]),
    ]
    for copy in copies:
        copy.start()
    for copy in copies:
        copy.wait()
    cum_ref[...] = running_sum(log_decay[...])
    b_t = b[...].astype(F32).T
    for k, shift in enumerate(ORDER):
        owner = (pos[0] + shift) & (NZ - 1)
        lasts = []
        for i in range(OWN):
            head = chunk * PER_CHUNK + owner * OWN + i
            cum = cum_ref[pl.ds(head, 1), :]
            last = jnp.broadcast_to(cum[:, W - 1 :], (1, W))
            high, low = split(b_t * jnp.exp(last - cum))
            x_head = x[:, pl.ds(pl.multiple_of(head * W, W), W)]
            state = jnp.dot(high, x_head, preferred_element_type=F32)
            state += jnp.dot(low, x_head, preferred_element_type=F32)
            outs[k][i * W : (i + 1) * W, :] = state
            lasts.append(last)
        outs[k][ROWS:, :] = decay_tile(lasts)


def row_total_kernel(pos, *refs):
    parts, out = refs[:NZ], refs[NZ]
    places = [(pos[0] - shift) & (NZ - 1) for shift in ORDER]
    totals = []
    for i in range(OWN):
        logs = [part[ROWS + i : ROWS + i + 1, :] for part in parts]
        total = jnp.zeros((W, W), F32)
        for k in range(NZ):
            after = jnp.zeros((1, W), F32)
            for j in range(NZ):
                if j != k:
                    after += jnp.where(places[j] > places[k], logs[j], 0.0)
            total += jnp.exp(after) * parts[k][i * W : (i + 1) * W, :]
        out[i * W : (i + 1) * W, :] = total
        totals.append(sum(logs))
    out[ROWS:, :] = decay_tile(totals)


def plane_kernel(pos, *refs):
    parts, plane, before = refs[:NY], refs[NY], refs[NY + 1]
    places = [pos[1] ^ k for k in range(NY)]
    plane_logs, before_logs = [], []
    for i in range(OWN):
        logs = [part[ROWS + i : ROWS + i + 1, :] for part in parts]
        total = jnp.zeros((W, W), F32)
        earlier = jnp.zeros((W, W), F32)
        to_row = jnp.zeros((1, W), F32)
        for k in range(NY):
            after = jnp.zeros((1, W), F32)
            between = jnp.zeros((1, W), F32)
            for j in range(NY):
                if j != k:
                    later = jnp.where(places[j] > places[k], logs[j], 0.0)
                    after += later
                    between += jnp.where(places[j] < pos[1], later, 0.0)
            piece = parts[k][i * W : (i + 1) * W, :]
            total += jnp.exp(after) * piece
            if k > 0:
                mine = places[k] < pos[1]
                earlier += jnp.where(mine, jnp.exp(between), 0.0) * piece
                to_row += jnp.where(mine, logs[k], 0.0)
        plane[i * W : (i + 1) * W, :] = total
        before[i * W : (i + 1) * W, :] = earlier
        plane_logs.append(sum(logs))
        before_logs.append(to_row)
    plane[ROWS:, :] = decay_tile(plane_logs)
    before[ROWS:, :] = decay_tile(before_logs)


def entering_kernel(pos, *refs):
    planes, before = refs[: NX - 1], refs[NX - 1]
    parts = refs[NX : NX + NZ]
    outs = refs[NX + NZ : NX + 2 * NZ]
    ordered, entering = refs[NX + 2 * NZ :]
    for k, shift in enumerate(ORDER):
        ordered[(pos[0] - shift) & (NZ - 1)] = parts[k][...]
    for i in range(OWN):
        carry = jnp.zeros((W, W), F32)
        logs = [plane[ROWS + i : ROWS + i + 1, :] for plane in planes]
        for k in range(1, NX):
            after = jnp.zeros((1, W), F32)
            for j in range(1, NX):
                if j != k:
                    between = jnp.logical_and(pos[2] ^ j > pos[2] ^ k, pos[2] ^ j < pos[2])
                    after += jnp.where(between, logs[j - 1], 0.0)
            weight = jnp.where(pos[2] ^ k < pos[2], jnp.exp(after), 0.0)
            carry += weight * planes[k - 1][i * W : (i + 1) * W, :]
        carry = jnp.exp(before[ROWS + i : ROWS + i + 1, :]) * carry
        carry += before[i * W : (i + 1) * W, :]
        for place in range(NZ):
            entering[place, i * W : (i + 1) * W, :] = carry
            if place < NZ - 1:
                decay = jnp.exp(ordered[place, ROWS + i : ROWS + i + 1, :])
                carry = decay * carry + ordered[place, i * W : (i + 1) * W, :]
    for k, shift in enumerate(ORDER):
        outs[k][...] = entering[(pos[0] + shift) & (NZ - 1)]


def inside_kernel(skip, x, z, b, c, log_decay, gain, fixed, slope, read, gain_out):
    read[...] = c[...]
    gain_out[...] = gain[...]
    lower = lower_mask()
    logs = log_decay[...]
    cum = running_sum(logs)
    cum_t = lax.dot_general(
        jnp.where(lower, 1.0, 0.0), logs, (((1,), (1,)), ((), ())),
        precision=HIGHEST, preferred_element_type=F32,
    )
    scores = lax.dot_general(c[...], b[...], (((1,), (1,)), ((), ())), preferred_element_type=F32)
    for head in range(HEADS):
        at = slice(head * W, (head + 1) * W)
        column = cum_t[:, head : head + 1]
        differ = column - cum[head : head + 1, :]
        within = jnp.where(lower, jnp.exp(jnp.where(lower, differ, 0.0)), 0.0)
        x_head = x[:, at]
        inner = jnp.dot((within * scores).astype(BF16), x_head, preferred_element_type=F32)
        gate = z[:, at].astype(F32)
        gate = gate / (1.0 + jnp.exp(-gate))
        fixed[:, at] = (inner + skip[head] * x_head.astype(F32)) * gate
        slope[:, at] = jnp.exp(column) * gate


def finish_kernel(shifts, last, pos, *refs):
    count = len(shifts)
    states, refs = refs[:count], refs[count:]
    read, fixed, slope, gain, w_hbm = refs[:5]
    if last:
        so_far, mine, other, normed, w, sems, tile = refs[5:]
    else:
        total, normed, w, sems = refs[5:]
    owners = [(pos[0] - shift) & (NZ - 1) for shift in shifts]
    copies = []
    for k, owner in enumerate(owners):
        rows = pl.ds(pl.multiple_of(owner * ROWS, ROWS), ROWS)
        copies.append(
            pltpu.make_async_copy(w_hbm.at[rows, :], w.at[k * ROWS : (k + 1) * ROWS, :], sems.at[k])
        )
        copies[k].start()
    for k, owner in enumerate(owners):
        for i in range(OWN):
            head = owner * OWN + i
            high, low = split(states[k][i * W : (i + 1) * W, :])
            carried = jnp.dot(read[...], high, preferred_element_type=F32)
            carried += jnp.dot(read[...], low, preferred_element_type=F32)
            at = pl.ds(pl.multiple_of(head * W, W), W)
            gated = fixed[:, at] + slope[:, at] * carried
            meansq = jnp.mean(gated * gated, axis=-1, keepdims=True)
            value = gated * lax.rsqrt(meansq + 1e-05) * gain[pl.ds(head, 1), :]
            place = k * ROWS + i * W
            normed[:, place : place + W] = value.astype(BF16)
    for copy in copies:
        copy.wait()
    for at in range(0, w.shape[1], TILE):
        columns = slice(at, at + TILE)
        part = jnp.dot(normed[...], w[:, columns], preferred_element_type=F32)
        if last:
            half = W // 2
            near = pl.ds(pl.multiple_of(pos[3] * half, half), half)
            far = pl.ds(pl.multiple_of((1 - pos[3]) * half, half), half)
            tile[...] = so_far[:, columns] + part
            mine[:, columns] = tile[near, :]
            other[:, columns] = tile[far, :]
        else:
            total[:, columns] = part


def call(kernel, outs, specs, scratch=(), flops=0, moved=0, name=None):
    return pl.pallas_call(
        kernel,
        out_shape=outs,
        in_specs=specs,
        out_specs=jax.tree.map(lambda _: VMEM, outs),
        scratch_shapes=scratch,
        compiler_params=pltpu.CompilerParams(vmem_limit_bytes=24 * 1024 * 1024),
        cost_estimate=pl.CostEstimate(flops=flops, bytes_accessed=moved, transcendentals=0),
        name=name,
    )


def shaped(*shape, dtype=F32):
    return jax.ShapeDtypeStruct(shape, dtype)


def per_device(x_in, z_in, b_in, c_in, log_decay, d_skip, norm_gain, w_out):
    index = lax.axis_index("ctx")
    pos = jnp.stack([index % NZ, index // NZ % NY, index // (NZ * NY), lax.axis_index("tp")]).astype(jnp.int32)
    x = x_in.reshape(W, HEADS * W)
    message = [shaped(MSG, W)] * NZ
    kept = {}
    for chunk in range(CHUNKS):
        kept[chunk] = call(
            functools.partial(local_state_kernel, chunk), message, [SMEM, VMEM, HBM, HBM],
            [
                pltpu.VMEM((HEADS, W), F32), pltpu.VMEM((W, W), BF16),
                pltpu.VMEM((HEADS, W), F32), pltpu.SemaphoreType.DMA((2,)),
            ], moved=1 << 20, name=f"local_state_{chunk}",
        )(pos, x, b_in, log_decay)
    z = z_in.reshape(W, HEADS * W)
    fixed, slope, read, gain = call(
        inside_kernel,
        [shaped(W, HEADS * W), shaped(W, HEADS * W), shaped(W, W, dtype=BF16), shaped(HEADS, W)],
        [SMEM] + [VMEM] * 6, moved=8 << 20, name="inside",
    )(d_skip, x, z, b_in, c_in, log_decay, norm_gain)

    def along_z(parts):
        return [parts[0]] + [
            lax.ppermute(part, "ctx", z_shift(shift)) for part, shift in zip(parts[1:], ORDER[1:])
        ]

    parts, totals, back, states = {}, {}, {}, {}
    for chunk in range(CHUNKS):
        parts[chunk] = along_z(kept[chunk])
        totals[chunk] = call(
            row_total_kernel, shaped(MSG, W), [SMEM] + [VMEM] * NZ, name=f"row_total_{chunk}"
        )(pos, *parts[chunk])
    totals[0], fixed, slope, read, gain = lax.optimization_barrier(
        (totals[0], fixed, slope, read, gain)
    )
    for chunk in range(CHUNKS):
        total = totals[chunk]
        rows = [total] + [lax.ppermute(total, "ctx", partners(NZ, k)) for k in range(1, NY)]
        plane, before = call(
            plane_kernel, [shaped(MSG, W)] * 2, [SMEM] + [VMEM] * NY, name=f"plane_{chunk}"
        )(pos, *rows)
        planes = [lax.ppermute(plane, "ctx", partners(NY * NZ, k)) for k in range(1, NX)]
        back[chunk] = call(
            entering_kernel, [shaped(ROWS, W)] * NZ, [SMEM] + [VMEM] * (NX + NZ),
            [pltpu.VMEM((NZ, MSG, W), F32), pltpu.VMEM((NZ, ROWS, W), F32)], name=f"entering_{chunk}",
        )(pos, *planes, before, *parts[chunk])
        states[chunk] = along_z(back[chunk])
    width = w_out.shape[1]

    def finish(shifts, parts, last, outs, extra):
        rows = len(shifts) * ROWS
        return call(
            functools.partial(finish_kernel, shifts, last), outs,
            [SMEM] + [VMEM] * (len(shifts) + 4) + [HBM] + [VMEM] * len(extra),
            [
                pltpu.VMEM((W, rows), BF16), pltpu.VMEM((rows, width), BF16),
                pltpu.SemaphoreType.DMA((len(shifts),)),
            ] + ([pltpu.VMEM((W, TILE), F32)] if last else []),
            name="finish_late" if last else "finish_early",
        )(pos, *parts, read, fixed, slope, gain, w_out, *extra)

    so_far = finish(ORDER[:EARLY], states[0][:EARLY], False, shaped(W, width), [])
    mine, other = finish(
        ORDER[EARLY:], states[0][EARLY:], True, [shaped(W // 2, width)] * 2, [so_far]
    )
    return (mine + lax.ppermute(other, "tp", [(0, 1), (1, 0)])).astype(BF16)


def solution(mesh):
    return jax.shard_map(
        per_device,
        mesh=mesh,
        in_specs=(
            P("ctx", "tp", None),
            P("ctx", "tp", None),
            P("ctx", None),
            P("ctx", None),
            P("tp", "ctx"),
            P("tp"),
            P("tp", None),
            P("tp", None),
        ),
        out_specs=P(("ctx", "tp"), None),
        check_vma=False,
    )
```

```python
import functools

import jax
import jax.numpy as jnp
from jax import lax
from jax.experimental import pallas as pl
from jax.experimental.pallas import tpu as pltpu
from jax.sharding import PartitionSpec as P

F32 = jnp.float32
BF16 = jnp.bfloat16
HIGHEST = lax.Precision.HIGHEST
NX, NY, NZ = 4, 4, 8
PAIRS = NZ // 2
HEADS = 16
W = 128
GROUPS = 2
HALF = HEADS // GROUPS // 2
ROWS = HALF * W
TILE = 512
WORK = 10**10
VMEM = pl.BlockSpec(memory_space=pltpu.VMEM)
SMEM = pl.BlockSpec(memory_space=pltpu.SMEM)


def partners(stride, k):
    return [(i, i ^ (stride * k)) for i in range(NX * NY * NZ)]


def split(value):
    high = value.astype(BF16)
    return high, (value - high.astype(F32)).astype(BF16)


def lower_mask():
    rows = lax.broadcasted_iota(jnp.int32, (W, W), 0)
    columns = lax.broadcasted_iota(jnp.int32, (W, W), 1)
    return rows >= columns


def running_sum(log_decay):
    upper = jnp.where(lower_mask(), 1.0, 0.0).T
    return jnp.dot(log_decay, upper, precision=HIGHEST, preferred_element_type=F32)


def decay_tile(rows):
    place = lax.broadcasted_iota(jnp.int32, (8, W), 0)
    tile = jnp.zeros((8, W), F32)
    for i, row in enumerate(rows):
        tile = jnp.where(place == i, jnp.broadcast_to(row, (8, W)), tile)
    return tile


def running_sum_t(log_decay):
    lower = jnp.where(lower_mask(), 1.0, 0.0)
    return lax.dot_general(
        lower, log_decay, (((1,), (1,)), ((), ())), precision=HIGHEST, preferred_element_type=F32
    )


def rows_of(index):
    return pl.ds(pl.multiple_of(index * W, W), W)


def local_state_kernel(group, pos, x, b, log_decay, keep, send, cum_ref):
    cum_ref[...] = running_sum(log_decay[...])
    b_t = b[...].astype(F32).T
    role = pos[0] & 1
    for out, side in ((send, 1 - role), (keep, role)):
        lasts = []
        for j in range(HALF):
            head = (group * 2 + side) * HALF + j
            cum = cum_ref[pl.ds(head, 1), :]
            last = jnp.broadcast_to(cum[:, W - 1 :], (1, W))
            parts = jnp.concatenate(split(b_t * jnp.exp(last - cum)), axis=1)
            x_head = x[:, rows_of(head)]
            out[j * W : (j + 1) * W, :] = jnp.dot(
                parts, jnp.concatenate([x_head, x_head]), preferred_element_type=F32
            )
            lasts.append(last)
        out[ROWS:, :] = decay_tile(lasts)


def pair_kernel(pos, keep, got, *outs):
    first = pos[0] & 1 == 0
    for m in range(PAIRS):
        j = (pos[0] >> 1) ^ m
        state, log = rows_of(j), pl.ds(ROWS + j, 1)
        earlier = jnp.where(first, keep[state, :], got[state, :])
        later = jnp.where(first, got[state, :], keep[state, :])
        decay = jnp.exp(jnp.where(first, got[log, :], keep[log, :]))
        outs[m][:W, :] = decay * earlier + later
        outs[m][W:, :] = decay_tile([keep[log, :] + got[log, :]])


def row_total_kernel(pos, *refs):
    parts, out = refs[:PAIRS], refs[PAIRS]
    places = [(pos[0] >> 1) ^ m for m in range(PAIRS)]
    logs = [part[W : W + 1, :] for part in parts]
    total = jnp.zeros((W, W), F32)
    for k in range(PAIRS):
        after = jnp.zeros((1, W), F32)
        for j in range(PAIRS):
            if j != k:
                after += jnp.where(places[j] > places[k], logs[j], 0.0)
        total += jnp.exp(after) * parts[k][:W, :]
    out[:W, :] = total
    out[W:, :] = decay_tile([sum(logs)])


def plane_kernel(pos, *refs):
    parts, plane, before = refs[:NY], refs[NY], refs[NY + 1]
    places = [pos[1] ^ k for k in range(NY)]
    logs = [part[W : W + 1, :] for part in parts]
    total = jnp.zeros((W, W), F32)
    earlier = jnp.zeros((W, W), F32)
    to_row = jnp.zeros((1, W), F32)
    for k in range(NY):
        after = jnp.zeros((1, W), F32)
        between = jnp.zeros((1, W), F32)
        for j in range(NY):
            if j != k:
                later = jnp.where(places[j] > places[k], logs[j], 0.0)
                after += later
                between += jnp.where(places[j] < pos[1], later, 0.0)
        piece = parts[k][:W, :]
        total += jnp.exp(after) * piece
        if k > 0:
            mine = places[k] < pos[1]
            earlier += jnp.where(mine, jnp.exp(between), 0.0) * piece
            to_row += jnp.where(mine, logs[k], 0.0)
    plane[:W, :] = total
    before[:W, :] = earlier
    plane[W:, :] = decay_tile([sum(logs)])
    before[W:, :] = decay_tile([to_row])


def entering_kernel(pos, *refs):
    planes, before = refs[: NX - 1], refs[NX - 1]
    parts = refs[NX : NX + PAIRS]
    outs = refs[NX + PAIRS : NX + 2 * PAIRS]
    ordered, entering = refs[NX + 2 * PAIRS :]
    for m in range(PAIRS):
        ordered[(pos[0] >> 1) ^ m] = parts[m][...]
    carry = jnp.zeros((W, W), F32)
    logs = [plane[W : W + 1, :] for plane in planes]
    for k in range(1, NX):
        after = jnp.zeros((1, W), F32)
        for j in range(1, NX):
            if j != k:
                between = jnp.logical_and(pos[2] ^ j > pos[2] ^ k, pos[2] ^ j < pos[2])
                after += jnp.where(between, logs[j - 1], 0.0)
        weight = jnp.where(pos[2] ^ k < pos[2], jnp.exp(after), 0.0)
        carry += weight * planes[k - 1][:W, :]
    carry = jnp.exp(before[W : W + 1, :]) * carry + before[:W, :]
    for place in range(PAIRS):
        entering[place] = carry
        if place < PAIRS - 1:
            carry = jnp.exp(ordered[place, W : W + 1, :]) * carry + ordered[place, :W, :]
    for m in range(PAIRS):
        outs[m][...] = entering[(pos[0] >> 1) ^ m]


def spread_kernel(pos, keep, got, *refs):
    carries, mine, send = refs[:PAIRS], refs[PAIRS], refs[PAIRS + 1]
    first = pos[0] & 1 == 0
    for m in range(PAIRS):
        j = (pos[0] >> 1) ^ m
        state, log = rows_of(j), pl.ds(ROWS + j, 1)
        carry = carries[m][...]
        decay = jnp.exp(jnp.where(first, keep[log, :], got[log, :]))
        after = decay * carry + jnp.where(first, keep[state, :], got[state, :])
        mine[state, :] = jnp.where(first, carry, after)
        send[state, :] = jnp.where(first, after, carry)


def inside_kernel(skip, x, z, b, c, log_decay, gain, fixed, slope, read, gain_out):
    read[...] = c[...]
    gain_out[...] = gain[...]
    lower = lower_mask()
    logs = log_decay[...]
    cum = running_sum(logs)
    cum_t = running_sum_t(logs)
    scores = lax.dot_general(c[...], b[...], (((1,), (1,)), ((), ())), preferred_element_type=F32)
    for head in range(HEADS):
        at = slice(head * W, (head + 1) * W)
        column = cum_t[:, head : head + 1]
        differ = column - cum[head : head + 1, :]
        within = jnp.where(lower, jnp.exp(jnp.where(lower, differ, 0.0)), 0.0)
        x_head = x[:, at]
        inner = jnp.dot((within * scores).astype(BF16), x_head, preferred_element_type=F32)
        gate = z[:, at].astype(F32)
        gate = gate / (1.0 + jnp.exp(-gate))
        fixed[:, at] = (inner + skip[head] * x_head.astype(F32)) * gate
        slope[:, at] = jnp.exp(column) * gate


def finish_kernel(group, sides, stage, pos, *refs):
    count = len(sides)
    states, refs = refs[:count], refs[count:]
    read, fixed, slope, gain, w = refs[:5]
    first_row = 0
    if stage == 0:
        total, w_next, normed, sem = refs[5:]
        fetch = pltpu.make_async_copy(w.at[w_next.shape[0] :, :], w_next, sem)
        fetch.start()
    elif stage == 1:
        so_far, total, normed = refs[5:]
        first_row = w.shape[0]
    else:
        so_far, mine, other, normed, tile = refs[5:]
        first_row = w.shape[0]
    role = pos[0] & 1
    bases = [(group * 2 + (1 - role if side else role)) * HALF for side in sides]
    twice = jnp.concatenate([read[...], read[...]], axis=1)
    for k, base in enumerate(bases):
        for i in range(0, HALF, 2):
            parts = [split(states[k][(i + n) * W : (i + n + 1) * W, :]) for n in range(2)]
            both = [jnp.concatenate(half, axis=1) for half in zip(*parts)]
            carried = jnp.dot(twice, jnp.concatenate(both), preferred_element_type=F32)
            for n in range(2):
                head = base + i + n
                at = rows_of(head)
                gated = fixed[:, at] + slope[:, at] * carried[:, n * W : (n + 1) * W]
                meansq = jnp.mean(gated * gated, axis=-1, keepdims=True)
                value = gated * lax.rsqrt(meansq + 1e-05) * gain[pl.ds(head, 1), :]
                place = k * ROWS + (i + n) * W
                normed[:, place : place + W] = value.astype(BF16)
    for at in range(0, w.shape[1], TILE):
        columns = slice(at, at + TILE)
        part = jnp.zeros((W, TILE), F32) if stage == 0 else so_far[:, columns]
        for k, base in enumerate(bases):
            rows = pl.ds(pl.multiple_of(base * W - first_row, ROWS), ROWS)
            part += jnp.dot(
                normed[:, k * ROWS : (k + 1) * ROWS], w[rows, columns], preferred_element_type=F32
            )
        if stage < 2:
            total[:, columns] = part
        else:
            half = W // 2
            tile[...] = part
            mine[:, columns] = tile[pl.ds(pl.multiple_of(pos[3] * half, half), half), :]
            other[:, columns] = tile[pl.ds(pl.multiple_of((1 - pos[3]) * half, half), half), :]
    if stage == 0:
        fetch.wait()


def call(kernel, outs, specs, scratch=(), name=None, grant=16, work=0):
    return pl.pallas_call(
        kernel,
        out_shape=outs,
        in_specs=specs,
        out_specs=jax.tree.map(lambda _: VMEM, outs),
        scratch_shapes=scratch,
        compiler_params=pltpu.CompilerParams(vmem_limit_bytes=grant * 1024 * 1024),
        cost_estimate=pl.CostEstimate(flops=work, bytes_accessed=0, transcendentals=0),
        name=name,
    )


def shaped(*shape, dtype=F32):
    return jax.ShapeDtypeStruct(shape, dtype)


def per_device(x_in, z_in, b_in, c_in, log_decay, d_skip, norm_gain, w_out):
    index = lax.axis_index("ctx")
    pos = jnp.stack([index % NZ, index // NZ % NY, index // (NZ * NY), lax.axis_index("tp")]).astype(jnp.int32)
    x = x_in.reshape(W, HEADS * W)
    width = w_out.shape[1]
    full, single = shaped(ROWS + 8, W), shaped(W + 8, W)
    keep, got, parts, totals, planes, mine, states = {}, {}, {}, {}, {}, {}, {}
    for g in range(GROUPS):
        keep[g], send = call(
            functools.partial(local_state_kernel, g), [full] * 2, [SMEM, VMEM, VMEM, VMEM],
            [pltpu.VMEM((HEADS, W), F32)], name=f"local_state_{g}",
        )(pos, x, b_in, log_decay)
        got[g] = lax.ppermute(send, "ctx", partners(1, 1))
    keep[1], z = lax.optimization_barrier((keep[1], z_in))
    fixed, slope, read, gain = call(
        inside_kernel,
        [shaped(W, HEADS * W), shaped(W, HEADS * W), shaped(W, W, dtype=BF16), shaped(HEADS, W)],
        [SMEM] + [VMEM] * 6, name="inside",
    )(d_skip, x, z.reshape(W, HEADS * W), b_in, c_in, log_decay, norm_gain)
    keep[0], fixed, slope, read, gain = lax.optimization_barrier(
        (keep[0], fixed, slope, read, gain)
    )
    for g in range(GROUPS):
        pair = call(pair_kernel, [single] * PAIRS, [SMEM, VMEM, VMEM], name=f"pair_{g}")(
            pos, keep[g], got[g]
        )
        parts[g] = [pair[0]] + [lax.ppermute(pair[m], "ctx", partners(2, m)) for m in range(1, PAIRS)]
    for g in range(GROUPS):
        total = call(
            row_total_kernel, single, [SMEM] + [VMEM] * PAIRS, name=f"row_total_{g}"
        )(pos, *parts[g])
        totals[g] = [total] + [lax.ppermute(total, "ctx", partners(NZ, k)) for k in range(1, NY)]
    for g in range(GROUPS):
        plane, before = call(
            plane_kernel, [single] * 2, [SMEM] + [VMEM] * NY, name=f"plane_{g}"
        )(pos, *totals[g])
        planes[g] = [lax.ppermute(plane, "ctx", partners(NY * NZ, k)) for k in range(1, NX)] + [before]
    for g in range(GROUPS):
        back = call(
            entering_kernel, [shaped(W, W)] * PAIRS, [SMEM] + [VMEM] * (NX + PAIRS),
            [pltpu.VMEM((PAIRS, W + 8, W), F32), pltpu.VMEM((PAIRS, W, W), F32)],
            name=f"entering_{g}", work=WORK,
        )(pos, *planes[g], *parts[g])
        states[g] = [back[0]] + [lax.ppermute(back[m], "ctx", partners(2, m)) for m in range(1, PAIRS)]
    for g in range(GROUPS):
        mine[g], send = call(
            spread_kernel, [shaped(ROWS, W)] * 2, [SMEM] + [VMEM] * (2 + PAIRS), name=f"spread_{g}"
        )(pos, keep[g], got[g], *states[g])
        states[g] = lax.ppermute(send, "ctx", partners(1, 1))

    def finish(group, sides, stage, parts, w, outs, extra):
        scratch = [pltpu.VMEM((W, len(sides) * ROWS), BF16)]
        scratch += [[pltpu.SemaphoreType.DMA(())], [], [pltpu.VMEM((W, TILE), F32)]][stage]
        return call(
            functools.partial(finish_kernel, group, sides, stage), outs,
            [SMEM] + [VMEM] * (len(sides) + 5 + len(extra)), scratch, name=f"finish_{stage}",
        )(pos, *parts, read, fixed, slope, gain, w, *extra)

    so_far, w = finish(
        0, (0, 1), 0, [mine[0], states[0]], w_out,
        [shaped(W, width), shaped(w_out.shape[0] // 2, width, dtype=BF16)], [],
    )
    so_far = finish(1, (0,), 1, [mine[1]], w, shaped(W, width), [so_far])
    near, far = finish(1, (1,), 2, [states[1]], w, [shaped(W // 2, width)] * 2, [so_far])
    return (near + lax.ppermute(far, "tp", [(0, 1), (1, 0)])).astype(BF16)


def solution(mesh):
    return jax.shard_map(
        per_device,
        mesh=mesh,
        in_specs=(
            P("ctx", "tp", None),
            P("ctx", "tp", None),
            P("ctx", None),
            P("ctx", None),
            P("tp", "ctx"),
            P("tp"),
            P("tp", None),
            P("tp", None),
        ),
        out_specs=P(("ctx", "tp"), None),
        check_vma=False,
    )
```

```python
import functools

import jax
import jax.numpy as jnp
from jax import lax
from jax.experimental import pallas as pl
from jax.experimental.pallas import tpu as pltpu
from jax.sharding import PartitionSpec as P

F32 = jnp.float32
BF16 = jnp.bfloat16
HIGHEST = lax.Precision.HIGHEST
NX, NY, NZ = 4, 4, 8
PAIRS = NZ // 2
HEADS = 16
W = 128
GROUPS = 2
HALF = HEADS // GROUPS // 2
ROWS = HALF * W
TILE = 512
WORK = 10**10
UP, DOWN, ACROSS = (0, 3, 2, 1), (0, 3, 2, 1), (0, 1, 2, 3)
VMEM = pl.BlockSpec(memory_space=pltpu.VMEM)
SMEM = pl.BlockSpec(memory_space=pltpu.SMEM)


def partners(stride, k):
    return [(i, i ^ (stride * k)) for i in range(NX * NY * NZ)]


def split(value):
    high = value.astype(BF16)
    return high, (value - high.astype(F32)).astype(BF16)


def lower_mask():
    rows = lax.broadcasted_iota(jnp.int32, (W, W), 0)
    columns = lax.broadcasted_iota(jnp.int32, (W, W), 1)
    return rows >= columns


def running_sum(log_decay):
    upper = jnp.where(lower_mask(), 1.0, 0.0).T
    return jnp.dot(log_decay, upper, precision=HIGHEST, preferred_element_type=F32)


def decay_tile(rows):
    place = lax.broadcasted_iota(jnp.int32, (8, W), 0)
    tile = jnp.zeros((8, W), F32)
    for i, row in enumerate(rows):
        tile = jnp.where(place == i, jnp.broadcast_to(row, (8, W)), tile)
    return tile


def running_sum_t(log_decay):
    lower = jnp.where(lower_mask(), 1.0, 0.0)
    return lax.dot_general(
        lower, log_decay, (((1,), (1,)), ((), ())), precision=HIGHEST, preferred_element_type=F32
    )


def position():
    index = lax.axis_index("ctx")
    return index & (NZ - 1), (index >> 3) & (NY - 1), index >> 5, lax.axis_index("tp")


def rows_of(index):
    return pl.ds(pl.multiple_of(index * W, W), W)


def local_state_kernel(group, x, b, log_decay, keep, send, cum_ref):
    pos = position()
    cum_ref[...] = running_sum(log_decay[...])
    b_t = b[...].astype(F32).T
    role = pos[0] & 1
    for out, side in ((send, 1 - role), (keep, role)):
        lasts = []
        for j in range(HALF):
            head = (group * 2 + side) * HALF + j
            cum = cum_ref[pl.ds(head, 1), :]
            last = jnp.broadcast_to(cum[:, W - 1 :], (1, W))
            parts = jnp.concatenate(split(b_t * jnp.exp(last - cum)), axis=1)
            x_head = x[:, rows_of(head)]
            out[j * W : (j + 1) * W, :] = jnp.dot(
                parts, jnp.concatenate([x_head, x_head]), preferred_element_type=F32
            )
            lasts.append(last)
        out[ROWS:, :] = decay_tile(lasts)


def pair_kernel(keep, got, *outs):
    pos = position()
    first = pos[0] & 1 == 0
    for k, m in enumerate(UP):
        j = (pos[0] >> 1) ^ m
        state, log = rows_of(j), pl.ds(ROWS + j, 1)
        earlier = jnp.where(first, keep[state, :], got[state, :])
        later = jnp.where(first, got[state, :], keep[state, :])
        decay = jnp.exp(jnp.where(first, got[log, :], keep[log, :]))
        outs[k][:W, :] = decay * earlier + later
        outs[k][W:, :] = decay_tile([keep[log, :] + got[log, :]])


def row_total_kernel(*refs):
    pos = position()
    parts, out = refs[:PAIRS], refs[PAIRS]
    places = [(pos[0] >> 1) ^ m for m in UP]
    logs = [part[W : W + 1, :] for part in parts]
    total = jnp.zeros((W, W), F32)
    for k in range(PAIRS):
        after = jnp.zeros((1, W), F32)
        for j in range(PAIRS):
            if j != k:
                after += jnp.where(places[j] > places[k], logs[j], 0.0)
        total += jnp.exp(after) * parts[k][:W, :]
    out[:W, :] = total
    out[W:, :] = decay_tile([sum(logs)])


def plane_kernel(*refs):
    pos = position()
    parts, plane, before = refs[:NY], refs[NY], refs[NY + 1]
    places = [pos[1] ^ m for m in ACROSS]
    logs = [part[W : W + 1, :] for part in parts]
    total = jnp.zeros((W, W), F32)
    earlier = jnp.zeros((W, W), F32)
    to_row = jnp.zeros((1, W), F32)
    for k in range(NY):
        after = jnp.zeros((1, W), F32)
        between = jnp.zeros((1, W), F32)
        for j in range(NY):
            if j != k:
                later = jnp.where(places[j] > places[k], logs[j], 0.0)
                after += later
                between += jnp.where(places[j] < pos[1], later, 0.0)
        piece = parts[k][:W, :]
        total += jnp.exp(after) * piece
        if k > 0:
            mine = places[k] < pos[1]
            earlier += jnp.where(mine, jnp.exp(between), 0.0) * piece
            to_row += jnp.where(mine, logs[k], 0.0)
    plane[:W, :] = total
    before[:W, :] = earlier
    plane[W:, :] = decay_tile([sum(logs)])
    before[W:, :] = decay_tile([to_row])


def entering_kernel(*refs):
    pos = position()
    planes, before = refs[: NX - 1], refs[NX - 1]
    parts = refs[NX : NX + PAIRS]
    outs = refs[NX + PAIRS : NX + 2 * PAIRS]
    ordered, entering = refs[NX + 2 * PAIRS :]
    for k, m in enumerate(UP):
        ordered[(pos[0] >> 1) ^ m] = parts[k][...]
    carry = jnp.zeros((W, W), F32)
    logs = [plane[W : W + 1, :] for plane in planes]
    places = [pos[2] ^ m for m in ACROSS[1:]]
    for k in range(NX - 1):
        after = jnp.zeros((1, W), F32)
        for j in range(NX - 1):
            if j != k:
                between = jnp.logical_and(places[j] > places[k], places[j] < pos[2])
                after += jnp.where(between, logs[j], 0.0)
        weight = jnp.where(places[k] < pos[2], jnp.exp(after), 0.0)
        carry += weight * planes[k][:W, :]
    carry = jnp.exp(before[W : W + 1, :]) * carry + before[:W, :]
    for place in range(PAIRS):
        entering[place] = carry
        if place < PAIRS - 1:
            carry = jnp.exp(ordered[place, W : W + 1, :]) * carry + ordered[place, :W, :]
    for k, m in enumerate(DOWN):
        outs[k][...] = entering[(pos[0] >> 1) ^ m]


def spread_kernel(keep, got, *refs):
    pos = position()
    carries, mine, send = refs[:PAIRS], refs[PAIRS], refs[PAIRS + 1]
    first = pos[0] & 1 == 0
    for k, m in enumerate(DOWN):
        j = (pos[0] >> 1) ^ m
        state, log = rows_of(j), pl.ds(ROWS + j, 1)
        carry = carries[k][...]
        decay = jnp.exp(jnp.where(first, keep[log, :], got[log, :]))
        after = decay * carry + jnp.where(first, keep[state, :], got[state, :])
        mine[state, :] = jnp.where(first, carry, after)
        send[state, :] = jnp.where(first, after, carry)


def inside_kernel(skip, x, z, b, c, log_decay, gain, fixed, slope, read, gain_out):
    read[...] = c[...]
    gain_out[...] = gain[...]
    lower = lower_mask()
    logs = log_decay[...]
    cum = running_sum(logs)
    cum_t = running_sum_t(logs)
    scores = lax.dot_general(c[...], b[...], (((1,), (1,)), ((), ())), preferred_element_type=F32)
    for head in range(HEADS):
        at = slice(head * W, (head + 1) * W)
        column = cum_t[:, head : head + 1]
        differ = column - cum[head : head + 1, :]
        within = jnp.where(lower, jnp.exp(jnp.where(lower, differ, 0.0)), 0.0)
        x_head = x[:, at]
        inner = jnp.dot((within * scores).astype(BF16), x_head, preferred_element_type=F32)
        gate = z[:, at].astype(F32)
        gate = gate / (1.0 + jnp.exp(-gate))
        fixed[:, at] = (inner + skip[head] * x_head.astype(F32)) * gate
        slope[:, at] = jnp.exp(column) * gate


def finish_kernel(group, sides, stage, *refs):
    pos = position()
    count = len(sides)
    states, refs = refs[:count], refs[count:]
    read, fixed, slope, gain, w = refs[:5]
    first_row = 0
    if stage == 0:
        total, w_next, normed, sem = refs[5:]
        fetch = pltpu.make_async_copy(w.at[w_next.shape[0] :, :], w_next, sem)
        fetch.start()
    elif stage == 1:
        so_far, total, normed = refs[5:]
        first_row = w.shape[0]
    else:
        so_far, mine, other, normed, tile = refs[5:]
        first_row = w.shape[0]
    role = pos[0] & 1
    bases = [(group * 2 + (1 - role if side else role)) * HALF for side in sides]
    twice = jnp.concatenate([read[...], read[...]], axis=1)
    for k, base in enumerate(bases):
        for i in range(0, HALF, 2):
            parts = [split(states[k][(i + n) * W : (i + n + 1) * W, :]) for n in range(2)]
            both = [jnp.concatenate(half, axis=1) for half in zip(*parts)]
            carried = jnp.dot(twice, jnp.concatenate(both), preferred_element_type=F32)
            for n in range(2):
                head = base + i + n
                at = rows_of(head)
                gated = fixed[:, at] + slope[:, at] * carried[:, n * W : (n + 1) * W]
                meansq = jnp.mean(gated * gated, axis=-1, keepdims=True)
                value = gated * lax.rsqrt(meansq + 1e-05) * gain[pl.ds(head, 1), :]
                place = k * ROWS + (i + n) * W
                normed[:, place : place + W] = value.astype(BF16)
    for at in range(0, w.shape[1], TILE):
        columns = slice(at, at + TILE)
        part = jnp.zeros((W, TILE), F32) if stage == 0 else so_far[:, columns]
        for k, base in enumerate(bases):
            rows = pl.ds(pl.multiple_of(base * W - first_row, ROWS), ROWS)
            part += jnp.dot(
                normed[:, k * ROWS : (k + 1) * ROWS], w[rows, columns], preferred_element_type=F32
            )
        if stage < 2:
            total[:, columns] = part
        else:
            half = W // 2
            tile[...] = part
            mine[:, columns] = tile[pl.ds(pl.multiple_of(pos[3] * half, half), half), :]
            other[:, columns] = tile[pl.ds(pl.multiple_of((1 - pos[3]) * half, half), half), :]
    if stage == 0:
        fetch.wait()


def call(kernel, outs, specs, scratch=(), name=None, grant=16, work=0):
    return pl.pallas_call(
        kernel,
        out_shape=outs,
        in_specs=specs,
        out_specs=jax.tree.map(lambda _: VMEM, outs),
        scratch_shapes=scratch,
        compiler_params=pltpu.CompilerParams(vmem_limit_bytes=grant * 1024 * 1024),
        cost_estimate=pl.CostEstimate(flops=work, bytes_accessed=0, transcendentals=0),
        name=name,
    )


def shaped(*shape, dtype=F32):
    return jax.ShapeDtypeStruct(shape, dtype)


def exchange(values, stride, order):
    return [values[0]] + [
        lax.ppermute(value, "ctx", partners(stride, m)) for value, m in zip(values[1:], order[1:])
    ]


def per_device(x_in, z_in, b_in, c_in, log_decay, d_skip, norm_gain, w_out):
    x = x_in.reshape(W, HEADS * W)
    width = w_out.shape[1]
    full, single = shaped(ROWS + 8, W), shaped(W + 8, W)
    keep, got, parts, totals, planes, mine, states = {}, {}, {}, {}, {}, {}, {}
    for g in range(GROUPS):
        keep[g], send = call(
            functools.partial(local_state_kernel, g), [full] * 2, [VMEM] * 3,
            [pltpu.VMEM((HEADS, W), F32)], name=f"local_state_{g}",
        )(x, b_in, log_decay)
        got[g] = lax.ppermute(send, "ctx", partners(1, 1))
    keep[1], z = lax.optimization_barrier((keep[1], z_in))
    fixed, slope, read, gain = call(
        inside_kernel,
        [shaped(W, HEADS * W), shaped(W, HEADS * W), shaped(W, W, dtype=BF16), shaped(HEADS, W)],
        [SMEM] + [VMEM] * 6, name="inside",
    )(d_skip, x, z.reshape(W, HEADS * W), b_in, c_in, log_decay, norm_gain)
    keep[0], fixed, slope, read, gain = lax.optimization_barrier(
        (keep[0], fixed, slope, read, gain)
    )
    for g in range(GROUPS):
        pair = call(pair_kernel, [single] * PAIRS, [VMEM] * 2, name=f"pair_{g}")(
            keep[g], got[g]
        )
        parts[g] = exchange(pair, 2, UP)
    for g in range(GROUPS):
        total = call(
            row_total_kernel, single, [VMEM] * PAIRS, name=f"row_total_{g}"
        )(*parts[g])
        totals[g] = exchange([total] * NY, NZ, ACROSS)
    for g in range(GROUPS):
        plane, before = call(
            plane_kernel, [single] * 2, [VMEM] * NY, name=f"plane_{g}"
        )(*totals[g])
        planes[g] = exchange([plane] * NX, NY * NZ, ACROSS)[1:] + [before]
    for g in range(GROUPS):
        back = call(
            entering_kernel, [shaped(W, W)] * PAIRS, [VMEM] * (NX + PAIRS),
            [pltpu.VMEM((PAIRS, W + 8, W), F32), pltpu.VMEM((PAIRS, W, W), F32)],
            name=f"entering_{g}", work=WORK,
        )(*planes[g], *parts[g])
        states[g] = exchange(back, 2, DOWN)
    for g in range(GROUPS):
        mine[g], send = call(
            spread_kernel, [shaped(ROWS, W)] * 2, [VMEM] * (2 + PAIRS), name=f"spread_{g}"
        )(keep[g], got[g], *states[g])
        states[g] = lax.ppermute(send, "ctx", partners(1, 1))

    def finish(group, sides, stage, parts, w, outs, extra):
        scratch = [pltpu.VMEM((W, len(sides) * ROWS), BF16)]
        scratch += [[pltpu.SemaphoreType.DMA(())], [], [pltpu.VMEM((W, TILE), F32)]][stage]
        return call(
            functools.partial(finish_kernel, group, sides, stage), outs,
            [VMEM] * (len(sides) + 5 + len(extra)), scratch, name=f"finish_{stage}",
        )(*parts, read, fixed, slope, gain, w, *extra)

    so_far, w = finish(
        0, (0, 1), 0, [mine[0], states[0]], w_out,
        [shaped(W, width), shaped(w_out.shape[0] // 2, width, dtype=BF16)], [],
    )
    so_far = finish(1, (0,), 1, [mine[1]], w, shaped(W, width), [so_far])
    near, far = finish(1, (1,), 2, [states[1]], w, [shaped(W // 2, width)] * 2, [so_far])
    return (near + lax.ppermute(far, "tp", [(0, 1), (1, 0)])).astype(BF16)


def solution(mesh):
    return jax.shard_map(
        per_device,
        mesh=mesh,
        in_specs=(
            P("ctx", "tp", None),
            P("ctx", "tp", None),
            P("ctx", None),
            P("ctx", None),
            P("tp", "ctx"),
            P("tp"),
            P("tp", None),
            P("tp", None),
        ),
        out_specs=P(("ctx", "tp"), None),
        check_vma=False,
    )
```

```python
import functools

import jax
import jax.numpy as jnp
from jax import lax
from jax.experimental import pallas as pl
from jax.experimental.pallas import tpu as pltpu
from jax.sharding import PartitionSpec as P

F32 = jnp.float32
BF16 = jnp.bfloat16
HIGHEST = lax.Precision.HIGHEST
NX, NY, NZ = 4, 4, 8
PAIRS = NZ // 2
HEADS = 16
W = 128
GROUPS = 2
HALF = HEADS // GROUPS // 2
ROWS = HALF * W
TILE = 512
WORK = 10**10
UP, DOWN, ACROSS = (0, 3, 2, 1), (0, 3, 2, 1), (0, 1, 2, 3)
VMEM = pl.BlockSpec(memory_space=pltpu.VMEM)
SMEM = pl.BlockSpec(memory_space=pltpu.SMEM)


def partners(stride, k):
    return [(i, i ^ (stride * k)) for i in range(NX * NY * NZ)]


def split(value):
    high = value.astype(BF16)
    return high, (value - high.astype(F32)).astype(BF16)


def lower_mask():
    rows = lax.broadcasted_iota(jnp.int32, (W, W), 0)
    columns = lax.broadcasted_iota(jnp.int32, (W, W), 1)
    return rows >= columns


def running_sum(log_decay, lower):
    return lax.dot_general(
        log_decay, lower, (((1,), (1,)), ((), ())), precision=HIGHEST, preferred_element_type=F32
    )


def decay_tile(rows):
    place = lax.broadcasted_iota(jnp.int32, (8, W), 0)
    tile = jnp.zeros((8, W), F32)
    for i, row in enumerate(rows):
        tile = jnp.where(place == i, jnp.broadcast_to(row, (8, W)), tile)
    return tile


def running_sum_t(log_decay, lower):
    return lax.dot_general(
        lower, log_decay, (((1,), (1,)), ((), ())), precision=HIGHEST, preferred_element_type=F32
    )


def lower_kernel(out):
    out[...] = jnp.where(lower_mask(), 1.0, 0.0)


def position():
    index = lax.axis_index("ctx")
    return index & (NZ - 1), (index >> 3) & (NY - 1), index >> 5, lax.axis_index("tp")


def rows_of(index):
    return pl.ds(pl.multiple_of(index * W, W), W)


def local_state_kernel(group, lower, x, b, log_decay, keep, send, cum_ref):
    pos = position()
    cum_ref[...] = running_sum(log_decay[...], lower[...])
    b_t = b[...].astype(F32).T
    role = pos[0] & 1
    for out, side in ((send, 1 - role), (keep, role)):
        lasts = []
        for j in range(HALF):
            head = (group * 2 + side) * HALF + j
            cum = cum_ref[pl.ds(head, 1), :]
            last = jnp.broadcast_to(cum[:, W - 1 :], (1, W))
            parts = jnp.concatenate(split(b_t * jnp.exp(last - cum)), axis=1)
            x_head = x[:, rows_of(head)]
            out[j * W : (j + 1) * W, :] = jnp.dot(
                parts, jnp.concatenate([x_head, x_head]), preferred_element_type=F32
            )
            lasts.append(last)
        out[ROWS:, :] = decay_tile(lasts)


def pair_kernel(keep, got, *outs):
    pos = position()
    first = pos[0] & 1 == 0
    for k, m in enumerate(UP):
        j = (pos[0] >> 1) ^ m
        state, log = rows_of(j), pl.ds(ROWS + j, 1)
        earlier = jnp.where(first, keep[state, :], got[state, :])
        later = jnp.where(first, got[state, :], keep[state, :])
        decay = jnp.exp(jnp.where(first, got[log, :], keep[log, :]))
        outs[k][:W, :] = decay * earlier + later
        outs[k][W:, :] = decay_tile([keep[log, :] + got[log, :]])


def row_total_kernel(*refs):
    pos = position()
    parts, out = refs[:PAIRS], refs[PAIRS]
    places = [(pos[0] >> 1) ^ m for m in UP]
    logs = [part[W : W + 1, :] for part in parts]
    total = jnp.zeros((W, W), F32)
    for k in range(PAIRS):
        after = jnp.zeros((1, W), F32)
        for j in range(PAIRS):
            if j != k:
                after += jnp.where(places[j] > places[k], logs[j], 0.0)
        total += jnp.exp(after) * parts[k][:W, :]
    out[:W, :] = total
    out[W:, :] = decay_tile([sum(logs)])


def plane_kernel(*refs):
    pos = position()
    parts, plane, before = refs[:NY], refs[NY], refs[NY + 1]
    places = [pos[1] ^ m for m in ACROSS]
    logs = [part[W : W + 1, :] for part in parts]
    total = jnp.zeros((W, W), F32)
    earlier = jnp.zeros((W, W), F32)
    to_row = jnp.zeros((1, W), F32)
    for k in range(NY):
        after = jnp.zeros((1, W), F32)
        between = jnp.zeros((1, W), F32)
        for j in range(NY):
            if j != k:
                later = jnp.where(places[j] > places[k], logs[j], 0.0)
                after += later
                between += jnp.where(places[j] < pos[1], later, 0.0)
        piece = parts[k][:W, :]
        total += jnp.exp(after) * piece
        if k > 0:
            mine = places[k] < pos[1]
            earlier += jnp.where(mine, jnp.exp(between), 0.0) * piece
            to_row += jnp.where(mine, logs[k], 0.0)
    plane[:W, :] = total
    before[:W, :] = earlier
    plane[W:, :] = decay_tile([sum(logs)])
    before[W:, :] = decay_tile([to_row])


def entering_kernel(*refs):
    pos = position()
    planes, before = refs[: NX - 1], refs[NX - 1]
    parts = refs[NX : NX + PAIRS]
    outs = refs[NX + PAIRS : NX + 2 * PAIRS]
    ordered, entering = refs[NX + 2 * PAIRS :]
    for k, m in enumerate(UP):
        ordered[(pos[0] >> 1) ^ m] = parts[k][...]
    carry = jnp.zeros((W, W), F32)
    logs = [plane[W : W + 1, :] for plane in planes]
    places = [pos[2] ^ m for m in ACROSS[1:]]
    for k in range(NX - 1):
        after = jnp.zeros((1, W), F32)
        for j in range(NX - 1):
            if j != k:
                between = jnp.logical_and(places[j] > places[k], places[j] < pos[2])
                after += jnp.where(between, logs[j], 0.0)
        weight = jnp.where(places[k] < pos[2], jnp.exp(after), 0.0)
        carry += weight * planes[k][:W, :]
    carry = jnp.exp(before[W : W + 1, :]) * carry + before[:W, :]
    for place in range(PAIRS):
        entering[place] = carry
        if place < PAIRS - 1:
            carry = jnp.exp(ordered[place, W : W + 1, :]) * carry + ordered[place, :W, :]
    for k, m in enumerate(DOWN):
        outs[k][...] = entering[(pos[0] >> 1) ^ m]


def spread_kernel(keep, got, *refs):
    pos = position()
    carries, mine, send = refs[:PAIRS], refs[PAIRS], refs[PAIRS + 1]
    first = pos[0] & 1 == 0
    for k, m in enumerate(DOWN):
        j = (pos[0] >> 1) ^ m
        state, log = rows_of(j), pl.ds(ROWS + j, 1)
        carry = carries[k][...]
        decay = jnp.exp(jnp.where(first, keep[log, :], got[log, :]))
        after = decay * carry + jnp.where(first, keep[state, :], got[state, :])
        mine[state, :] = jnp.where(first, carry, after)
        send[state, :] = jnp.where(first, after, carry)


def inside_kernel(skip, ones, x, z, b, c, log_decay, gain, fixed, slope, read, gain_out):
    read[...] = c[...]
    gain_out[...] = gain[...]
    lower = lower_mask()
    logs = log_decay[...]
    cum = running_sum(logs, ones[...])
    cum_t = running_sum_t(logs, ones[...])
    scores = lax.dot_general(c[...], b[...], (((1,), (1,)), ((), ())), preferred_element_type=F32)
    for head in range(HEADS):
        at = slice(head * W, (head + 1) * W)
        column = cum_t[:, head : head + 1]
        differ = column - cum[head : head + 1, :]
        within = jnp.where(lower, jnp.exp(jnp.where(lower, differ, 0.0)), 0.0)
        x_head = x[:, at]
        inner = jnp.dot((within * scores).astype(BF16), x_head, preferred_element_type=F32)
        gate = z[:, at].astype(F32)
        gate = gate / (1.0 + jnp.exp(-gate))
        fixed[:, at] = (inner + skip[head] * x_head.astype(F32)) * gate
        slope[:, at] = jnp.exp(column) * gate


def finish_kernel(group, sides, stage, *refs):
    pos = position()
    count = len(sides)
    states, refs = refs[:count], refs[count:]
    read, fixed, slope, gain, w = refs[:5]
    first_row = 0
    if stage == 0:
        total, w_next, normed, sem = refs[5:]
        fetch = pltpu.make_async_copy(w.at[w_next.shape[0] :, :], w_next, sem)
        fetch.start()
    elif stage == 1:
        so_far, total, normed = refs[5:]
        first_row = w.shape[0]
    else:
        so_far, mine, other, normed, tile = refs[5:]
        first_row = w.shape[0]
    role = pos[0] & 1
    bases = [(group * 2 + (1 - role if side else role)) * HALF for side in sides]
    twice = jnp.concatenate([read[...], read[...]], axis=1)
    for k, base in enumerate(bases):
        for i in range(0, HALF, 2):
            parts = [split(states[k][(i + n) * W : (i + n + 1) * W, :]) for n in range(2)]
            both = [jnp.concatenate(half, axis=1) for half in zip(*parts)]
            carried = jnp.dot(twice, jnp.concatenate(both), preferred_element_type=F32)
            for n in range(2):
                head = base + i + n
                at = rows_of(head)
                gated = fixed[:, at] + slope[:, at] * carried[:, n * W : (n + 1) * W]
                meansq = jnp.mean(gated * gated, axis=-1, keepdims=True)
                value = gated * lax.rsqrt(meansq + 1e-05) * gain[pl.ds(head, 1), :]
                place = k * ROWS + (i + n) * W
                normed[:, place : place + W] = value.astype(BF16)
    for at in range(0, w.shape[1], TILE):
        columns = slice(at, at + TILE)
        part = jnp.zeros((W, TILE), F32) if stage == 0 else so_far[:, columns]
        for k, base in enumerate(bases):
            rows = pl.ds(pl.multiple_of(base * W - first_row, ROWS), ROWS)
            part += jnp.dot(
                normed[:, k * ROWS : (k + 1) * ROWS], w[rows, columns], preferred_element_type=F32
            )
        if stage < 2:
            total[:, columns] = part
        else:
            half = W // 2
            tile[...] = part
            mine[:, columns] = tile[pl.ds(pl.multiple_of(pos[3] * half, half), half), :]
            other[:, columns] = tile[pl.ds(pl.multiple_of((1 - pos[3]) * half, half), half), :]
    if stage == 0:
        fetch.wait()


def call(kernel, outs, specs, scratch=(), name=None, grant=16, work=0):
    return pl.pallas_call(
        kernel,
        out_shape=outs,
        in_specs=specs,
        out_specs=jax.tree.map(lambda _: VMEM, outs),
        scratch_shapes=scratch,
        compiler_params=pltpu.CompilerParams(vmem_limit_bytes=grant * 1024 * 1024),
        cost_estimate=pl.CostEstimate(flops=work, bytes_accessed=0, transcendentals=0),
        name=name,
    )


def shaped(*shape, dtype=F32):
    return jax.ShapeDtypeStruct(shape, dtype)


def exchange(values, stride, order):
    return [values[0]] + [
        lax.ppermute(value, "ctx", partners(stride, m)) for value, m in zip(values[1:], order[1:])
    ]


def per_device(x_in, z_in, b_in, c_in, log_decay, d_skip, norm_gain, w_out):
    lower = call(lower_kernel, shaped(W, W), [], name="lower", work=WORK)()
    lower, x_in, z_in, b_in, c_in, log_decay, d_skip, norm_gain = lax.optimization_barrier(
        (lower, x_in, z_in, b_in, c_in, log_decay, d_skip, norm_gain)
    )
    x = x_in.reshape(W, HEADS * W)
    width = w_out.shape[1]
    full, single = shaped(ROWS + 8, W), shaped(W + 8, W)
    keep, got, parts, totals, planes, mine, states = {}, {}, {}, {}, {}, {}, {}
    for g in range(GROUPS):
        keep[g], send = call(
            functools.partial(local_state_kernel, g), [full] * 2, [VMEM] * 4,
            [pltpu.VMEM((HEADS, W), F32)], name=f"local_state_{g}",
        )(lower, x, b_in, log_decay)
        got[g] = lax.ppermute(send, "ctx", partners(1, 1))
    keep[1], z = lax.optimization_barrier((keep[1], z_in))
    fixed, slope, read, gain = call(
        inside_kernel,
        [shaped(W, HEADS * W), shaped(W, HEADS * W), shaped(W, W, dtype=BF16), shaped(HEADS, W)],
        [SMEM] + [VMEM] * 7, name="inside",
    )(d_skip, lower, x, z.reshape(W, HEADS * W), b_in, c_in, log_decay, norm_gain)
    keep[0], fixed, slope, read, gain = lax.optimization_barrier(
        (keep[0], fixed, slope, read, gain)
    )
    for g in range(GROUPS):
        pair = call(pair_kernel, [single] * PAIRS, [VMEM] * 2, name=f"pair_{g}")(
            keep[g], got[g]
        )
        parts[g] = exchange(pair, 2, UP)
    for g in range(GROUPS):
        total = call(
            row_total_kernel, single, [VMEM] * PAIRS, name=f"row_total_{g}"
        )(*parts[g])
        totals[g] = exchange([total] * NY, NZ, ACROSS)
    for g in range(GROUPS):
        plane, before = call(
            plane_kernel, [single] * 2, [VMEM] * NY, name=f"plane_{g}"
        )(*totals[g])
        planes[g] = exchange([plane] * NX, NY * NZ, ACROSS)[1:] + [before]
    for g in range(GROUPS):
        back = call(
            entering_kernel, [shaped(W, W)] * PAIRS, [VMEM] * (NX + PAIRS),
            [pltpu.VMEM((PAIRS, W + 8, W), F32), pltpu.VMEM((PAIRS, W, W), F32)],
            name=f"entering_{g}", work=WORK,
        )(*planes[g], *parts[g])
        states[g] = exchange(back, 2, DOWN)
    for g in range(GROUPS):
        mine[g], send = call(
            spread_kernel, [shaped(ROWS, W)] * 2, [VMEM] * (2 + PAIRS), name=f"spread_{g}"
        )(keep[g], got[g], *states[g])
        states[g] = lax.ppermute(send, "ctx", partners(1, 1))

    def finish(group, sides, stage, parts, w, outs, extra):
        scratch = [pltpu.VMEM((W, len(sides) * ROWS), BF16)]
        scratch += [[pltpu.SemaphoreType.DMA(())], [], [pltpu.VMEM((W, TILE), F32)]][stage]
        return call(
            functools.partial(finish_kernel, group, sides, stage), outs,
            [VMEM] * (len(sides) + 5 + len(extra)), scratch, name=f"finish_{stage}",
        )(*parts, read, fixed, slope, gain, w, *extra)

    so_far, w = finish(
        0, (0, 1), 0, [mine[0], states[0]], w_out,
        [shaped(W, width), shaped(w_out.shape[0] // 2, width, dtype=BF16)], [],
    )
    so_far = finish(1, (0,), 1, [mine[1]], w, shaped(W, width), [so_far])
    near, far = finish(1, (1,), 2, [states[1]], w, [shaped(W // 2, width)] * 2, [so_far])
    return (near + lax.ppermute(far, "tp", [(0, 1), (1, 0)])).astype(BF16)


def solution(mesh):
    return jax.shard_map(
        per_device,
        mesh=mesh,
        in_specs=(
            P("ctx", "tp", None),
            P("ctx", "tp", None),
            P("ctx", None),
            P("ctx", None),
            P("tp", "ctx"),
            P("tp"),
            P("tp", None),
            P("tp", None),
        ),
        out_specs=P(("ctx", "tp"), None),
        check_vma=False,
    )
```

```python
import functools

import jax
import jax.numpy as jnp
from jax import lax
from jax.experimental import pallas as pl
from jax.experimental.pallas import tpu as pltpu
from jax.sharding import PartitionSpec as P

F32 = jnp.float32
BF16 = jnp.bfloat16
HIGHEST = lax.Precision.HIGHEST
NX, NY, NZ = 4, 4, 8
PAIRS = NZ // 2
HEADS = 16
W = 128
GROUPS = 2
HALF = HEADS // GROUPS // 2
ROWS = HALF * W
TILE = 512
WORK = 10**10
UP, DOWN, ACROSS = (0, 3, 2, 1), (0, 3, 2, 1), (0, 1, 2, 3)
VMEM = pl.BlockSpec(memory_space=pltpu.VMEM)
SMEM = pl.BlockSpec(memory_space=pltpu.SMEM)


def partners(stride, k):
    return [(i, i ^ (stride * k)) for i in range(NX * NY * NZ)]


def split(value):
    high = value.astype(BF16)
    return high, (value - high.astype(F32)).astype(BF16)


def lower_mask():
    rows = lax.broadcasted_iota(jnp.int32, (W, W), 0)
    columns = lax.broadcasted_iota(jnp.int32, (W, W), 1)
    return rows >= columns


def running_sum(log_decay, lower):
    return lax.dot_general(
        log_decay, lower, (((1,), (1,)), ((), ())), precision=HIGHEST, preferred_element_type=F32
    )


def decay_tile(rows):
    place = lax.broadcasted_iota(jnp.int32, (8, W), 0)
    tile = jnp.zeros((8, W), F32)
    for i, row in enumerate(rows):
        tile = jnp.where(place == i, jnp.broadcast_to(row, (8, W)), tile)
    return tile


def running_sum_t(log_decay, lower):
    return lax.dot_general(
        lower, log_decay, (((1,), (1,)), ((), ())), precision=HIGHEST, preferred_element_type=F32
    )


def lower_kernel(out):
    out[...] = jnp.where(lower_mask(), 1.0, 0.0)


def position():
    index = lax.axis_index("ctx")
    return index & (NZ - 1), (index >> 3) & (NY - 1), index >> 5, lax.axis_index("tp")


def rows_of(index):
    return pl.ds(pl.multiple_of(index * W, W), W)


def local_state_kernel(group, lower, x, b, log_decay, keep, send, cum_ref):
    pos = position()
    cum_ref[...] = running_sum(log_decay[...], lower[...])
    b_t = b[...].astype(F32).T
    role = pos[0] & 1
    for out, side in ((send, 1 - role), (keep, role)):
        lasts = []
        for j in range(HALF):
            head = (group * 2 + side) * HALF + j
            cum = cum_ref[pl.ds(head, 1), :]
            last = jnp.broadcast_to(cum[:, W - 1 :], (1, W))
            parts = jnp.concatenate(split(b_t * jnp.exp(last - cum)), axis=1)
            x_head = x[:, rows_of(head)]
            out[j * W : (j + 1) * W, :] = jnp.dot(
                parts, jnp.concatenate([x_head, x_head]), preferred_element_type=F32
            )
            lasts.append(last)
        out[ROWS:, :] = decay_tile(lasts)


def pair_kernel(keep, got, *outs):
    pos = position()
    first = pos[0] & 1 == 0
    for k, m in enumerate(UP):
        j = (pos[0] >> 1) ^ m
        state, log = rows_of(j), pl.ds(ROWS + j, 1)
        earlier = jnp.where(first, keep[state, :], got[state, :])
        later = jnp.where(first, got[state, :], keep[state, :])
        decay = jnp.exp(jnp.where(first, got[log, :], keep[log, :]))
        outs[k][:W, :] = decay * earlier + later
        outs[k][W:, :] = decay_tile([keep[log, :] + got[log, :]])


def row_total_kernel(*refs):
    pos = position()
    parts, out = refs[:PAIRS], refs[PAIRS]
    places = [(pos[0] >> 1) ^ m for m in UP]
    logs = [part[W : W + 1, :] for part in parts]
    total = jnp.zeros((W, W), F32)
    for k in range(PAIRS):
        after = jnp.zeros((1, W), F32)
        for j in range(PAIRS):
            if j != k:
                after += jnp.where(places[j] > places[k], logs[j], 0.0)
        total += jnp.exp(after) * parts[k][:W, :]
    out[:W, :] = total
    out[W:, :] = decay_tile([sum(logs)])


def plane_kernel(*refs):
    pos = position()
    parts, plane, before = refs[:NY], refs[NY], refs[NY + 1]
    places = [pos[1] ^ m for m in ACROSS]
    logs = [part[W : W + 1, :] for part in parts]
    total = jnp.zeros((W, W), F32)
    earlier = jnp.zeros((W, W), F32)
    to_row = jnp.zeros((1, W), F32)
    for k in range(NY):
        after = jnp.zeros((1, W), F32)
        between = jnp.zeros((1, W), F32)
        for j in range(NY):
            if j != k:
                later = jnp.where(places[j] > places[k], logs[j], 0.0)
                after += later
                between += jnp.where(places[j] < pos[1], later, 0.0)
        piece = parts[k][:W, :]
        total += jnp.exp(after) * piece
        if k > 0:
            mine = places[k] < pos[1]
            earlier += jnp.where(mine, jnp.exp(between), 0.0) * piece
            to_row += jnp.where(mine, logs[k], 0.0)
    plane[:W, :] = total
    before[:W, :] = earlier
    plane[W:, :] = decay_tile([sum(logs)])
    before[W:, :] = decay_tile([to_row])


def entering_kernel(*refs):
    pos = position()
    planes, before = refs[: NX - 1], refs[NX - 1]
    parts = refs[NX : NX + PAIRS]
    outs = refs[NX + PAIRS : NX + 2 * PAIRS]
    ordered, entering = refs[NX + 2 * PAIRS :]
    for k, m in enumerate(UP):
        ordered[(pos[0] >> 1) ^ m] = parts[k][...]
    carry = jnp.zeros((W, W), F32)
    logs = [plane[W : W + 1, :] for plane in planes]
    places = [pos[2] ^ m for m in ACROSS[1:]]
    for k in range(NX - 1):
        after = jnp.zeros((1, W), F32)
        for j in range(NX - 1):
            if j != k:
                between = jnp.logical_and(places[j] > places[k], places[j] < pos[2])
                after += jnp.where(between, logs[j], 0.0)
        weight = jnp.where(places[k] < pos[2], jnp.exp(after), 0.0)
        carry += weight * planes[k][:W, :]
    carry = jnp.exp(before[W : W + 1, :]) * carry + before[:W, :]
    for place in range(PAIRS):
        entering[place] = carry
        if place < PAIRS - 1:
            carry = jnp.exp(ordered[place, W : W + 1, :]) * carry + ordered[place, :W, :]
    for k, m in enumerate(DOWN):
        outs[k][...] = entering[(pos[0] >> 1) ^ m]


def spread_kernel(keep, got, *refs):
    pos = position()
    carries, mine, send = refs[:PAIRS], refs[PAIRS], refs[PAIRS + 1]
    first = pos[0] & 1 == 0
    for k, m in enumerate(DOWN):
        j = (pos[0] >> 1) ^ m
        state, log = rows_of(j), pl.ds(ROWS + j, 1)
        carry = carries[k][...]
        decay = jnp.exp(jnp.where(first, keep[log, :], got[log, :]))
        after = decay * carry + jnp.where(first, keep[state, :], got[state, :])
        mine[state, :] = jnp.where(first, carry, after)
        send[state, :] = jnp.where(first, after, carry)


def inside_kernel(skip, ones, x, z, b, c, log_decay, gain, fixed, slope, read, gain_out):
    read[...] = c[...]
    gain_out[...] = gain[...]
    lower = lower_mask()
    logs = log_decay[...]
    cum = running_sum(logs, ones[...])
    cum_t = running_sum_t(logs, ones[...])
    scores = lax.dot_general(c[...], b[...], (((1,), (1,)), ((), ())), preferred_element_type=F32)
    for head in range(HEADS):
        at = slice(head * W, (head + 1) * W)
        column = cum_t[:, head : head + 1]
        differ = column - cum[head : head + 1, :]
        within = jnp.where(lower, jnp.exp(jnp.where(lower, differ, 0.0)), 0.0)
        x_head = x[:, at]
        inner = jnp.dot((within * scores).astype(BF16), x_head, preferred_element_type=F32)
        gate = z[:, at].astype(F32)
        gate = gate / (1.0 + jnp.exp(-gate))
        fixed[:, at] = (inner + skip[head] * x_head.astype(F32)) * gate
        slope[:, at] = jnp.exp(column) * gate


def finish_kernel(group, sides, stage, *refs):
    pos = position()
    count = len(sides)
    states, refs = refs[:count], refs[count:]
    read, fixed, slope, gain, w = refs[:5]
    first_row = 0
    if stage == 0:
        total, w_next, normed, sem = refs[5:]
        fetch = pltpu.make_async_copy(w.at[w_next.shape[0] :, :], w_next, sem)
        fetch.start()
    elif stage == 1:
        so_far, total, normed = refs[5:]
        first_row = w.shape[0]
    else:
        so_far, total, normed = refs[5:]
        first_row = w.shape[0]
    role = pos[0] & 1
    bases = [(group * 2 + (1 - role if side else role)) * HALF for side in sides]
    tokens = slice(None)
    if stage >= 2:
        core = pos[3] if stage == 3 else 1 - pos[3]
        tokens = pl.ds(pl.multiple_of(core * (W // 2), W // 2), W // 2)
    twice = jnp.concatenate([read[tokens, :], read[tokens, :]], axis=1)
    for k, base in enumerate(bases):
        for i in range(0, HALF, 2):
            parts = [split(states[k][(i + n) * W : (i + n + 1) * W, :]) for n in range(2)]
            both = [jnp.concatenate(half, axis=1) for half in zip(*parts)]
            carried = jnp.dot(twice, jnp.concatenate(both), preferred_element_type=F32)
            for n in range(2):
                head = base + i + n
                at = rows_of(head)
                gated = fixed[tokens, at] + slope[tokens, at] * carried[:, n * W : (n + 1) * W]
                meansq = jnp.mean(gated * gated, axis=-1, keepdims=True)
                value = gated * lax.rsqrt(meansq + 1e-05) * gain[pl.ds(head, 1), :]
                place = k * ROWS + (i + n) * W
                normed[:, place : place + W] = value.astype(BF16)
    for at in range(0, w.shape[1], TILE):
        columns = slice(at, at + TILE)
        part = jnp.zeros((W, TILE), F32) if stage == 0 else so_far[tokens, columns]
        for k, base in enumerate(bases):
            rows = pl.ds(pl.multiple_of(base * W - first_row, ROWS), ROWS)
            part += jnp.dot(
                normed[:, k * ROWS : (k + 1) * ROWS], w[rows, columns], preferred_element_type=F32
            )
        total[:, columns] = part
    if stage == 0:
        fetch.wait()


def call(kernel, outs, specs, scratch=(), name=None, grant=16, work=0):
    return pl.pallas_call(
        kernel,
        out_shape=outs,
        in_specs=specs,
        out_specs=jax.tree.map(lambda _: VMEM, outs),
        scratch_shapes=scratch,
        compiler_params=pltpu.CompilerParams(vmem_limit_bytes=grant * 1024 * 1024),
        cost_estimate=pl.CostEstimate(flops=work, bytes_accessed=0, transcendentals=0),
        name=name,
    )


def shaped(*shape, dtype=F32):
    return jax.ShapeDtypeStruct(shape, dtype)


def exchange(values, stride, order):
    return [values[0]] + [
        lax.ppermute(value, "ctx", partners(stride, m)) for value, m in zip(values[1:], order[1:])
    ]


def per_device(x_in, z_in, b_in, c_in, log_decay, d_skip, norm_gain, w_out):
    lower = call(lower_kernel, shaped(W, W), [], name="lower", work=WORK)()
    lower, x_in, z_in, b_in, c_in, log_decay, d_skip, norm_gain = lax.optimization_barrier(
        (lower, x_in, z_in, b_in, c_in, log_decay, d_skip, norm_gain)
    )
    x = x_in.reshape(W, HEADS * W)
    width = w_out.shape[1]
    full, single = shaped(ROWS + 8, W), shaped(W + 8, W)
    keep, got, parts, totals, planes, mine, states = {}, {}, {}, {}, {}, {}, {}
    for g in range(GROUPS):
        keep[g], send = call(
            functools.partial(local_state_kernel, g), [full] * 2, [VMEM] * 4,
            [pltpu.VMEM((HEADS, W), F32)], name=f"local_state_{g}",
        )(lower, x, b_in, log_decay)
        got[g] = lax.ppermute(send, "ctx", partners(1, 1))
    keep[1], z = lax.optimization_barrier((keep[1], z_in))
    fixed, slope, read, gain = call(
        inside_kernel,
        [shaped(W, HEADS * W), shaped(W, HEADS * W), shaped(W, W, dtype=BF16), shaped(HEADS, W)],
        [SMEM] + [VMEM] * 7, name="inside",
    )(d_skip, lower, x, z.reshape(W, HEADS * W), b_in, c_in, log_decay, norm_gain)
    keep[0], fixed, slope, read, gain = lax.optimization_barrier(
        (keep[0], fixed, slope, read, gain)
    )
    for g in range(GROUPS):
        pair = call(pair_kernel, [single] * PAIRS, [VMEM] * 2, name=f"pair_{g}")(
            keep[g], got[g]
        )
        parts[g] = exchange(pair, 2, UP)
    for g in range(GROUPS):
        total = call(
            row_total_kernel, single, [VMEM] * PAIRS, name=f"row_total_{g}"
        )(*parts[g])
        totals[g] = exchange([total] * NY, NZ, ACROSS)
    for g in range(GROUPS):
        plane, before = call(
            plane_kernel, [single] * 2, [VMEM] * NY, name=f"plane_{g}"
        )(*totals[g])
        planes[g] = exchange([plane] * NX, NY * NZ, ACROSS)[1:] + [before]
    for g in range(GROUPS):
        back = call(
            entering_kernel, [shaped(W, W)] * PAIRS, [VMEM] * (NX + PAIRS),
            [pltpu.VMEM((PAIRS, W + 8, W), F32), pltpu.VMEM((PAIRS, W, W), F32)],
            name=f"entering_{g}", work=WORK,
        )(*planes[g], *parts[g])
        states[g] = exchange(back, 2, DOWN)
    for g in range(GROUPS):
        mine[g], send = call(
            spread_kernel, [shaped(ROWS, W)] * 2, [VMEM] * (2 + PAIRS), name=f"spread_{g}"
        )(keep[g], got[g], *states[g])
        states[g] = lax.ppermute(send, "ctx", partners(1, 1))

    def finish(group, sides, stage, parts, w, outs, extra):
        scratch = [pltpu.VMEM((W // 2 if stage >= 2 else W, len(sides) * ROWS), BF16)]
        scratch += [pltpu.SemaphoreType.DMA(())] if stage == 0 else []
        return call(
            functools.partial(finish_kernel, group, sides, stage), outs,
            [VMEM] * (len(sides) + 5 + len(extra)), scratch, name=f"finish_{stage}",
        )(*parts, read, fixed, slope, gain, w, *extra)

    so_far, w = finish(
        0, (0, 1), 0, [mine[0], states[0]], w_out,
        [shaped(W, width), shaped(w_out.shape[0] // 2, width, dtype=BF16)], [],
    )
    so_far = finish(1, (0,), 1, [mine[1]], w, shaped(W, width), [so_far])
    far = finish(1, (1,), 2, [states[1]], w, shaped(W // 2, width), [so_far])
    arrived = lax.ppermute(far, "tp", [(0, 1), (1, 0)])
    near = finish(1, (1,), 3, [states[1]], w, shaped(W // 2, width), [so_far])
    return (near + arrived).astype(BF16)


def solution(mesh):
    return jax.shard_map(
        per_device,
        mesh=mesh,
        in_specs=(
            P("ctx", "tp", None),
            P("ctx", "tp", None),
            P("ctx", None),
            P("ctx", None),
            P("tp", "ctx"),
            P("tp"),
            P("tp", None),
            P("tp", None),
        ),
        out_specs=P(("ctx", "tp"), None),
        check_vma=False,
    )
```

```python
import functools

import jax
import jax.numpy as jnp
from jax import lax
from jax.experimental import pallas as pl
from jax.experimental.pallas import tpu as pltpu
from jax.sharding import PartitionSpec as P

F32 = jnp.float32
BF16 = jnp.bfloat16
HIGHEST = lax.Precision.HIGHEST
NX, NY, NZ = 4, 4, 8
PAIRS = NZ // 2
HEADS = 16
W = 128
GROUPS = 2
HALF = HEADS // GROUPS // 2
ROWS = HALF * W
TILE = 512
WORK = 10**10
UP, DOWN, ACROSS = (0, 3, 2, 1), (0, 3, 2, 1), (0, 1, 2, 3)
VMEM = pl.BlockSpec(memory_space=pltpu.VMEM)
SMEM = pl.BlockSpec(memory_space=pltpu.SMEM)


def partners(stride, k):
    return [(i, i ^ (stride * k)) for i in range(NX * NY * NZ)]


def split(value):
    high = value.astype(BF16)
    return high, (value - high.astype(F32)).astype(BF16)


def lower_mask():
    rows = lax.broadcasted_iota(jnp.int32, (W, W), 0)
    columns = lax.broadcasted_iota(jnp.int32, (W, W), 1)
    return rows >= columns


def running_sum(log_decay, lower):
    return lax.dot_general(
        log_decay, lower, (((1,), (1,)), ((), ())), precision=HIGHEST, preferred_element_type=F32
    )


def decay_tile(rows):
    place = lax.broadcasted_iota(jnp.int32, (8, W), 0)
    tile = jnp.zeros((8, W), F32)
    for i, row in enumerate(rows):
        tile = jnp.where(place == i, jnp.broadcast_to(row, (8, W)), tile)
    return tile


def running_sum_t(log_decay, lower):
    return lax.dot_general(
        lower, log_decay, (((1,), (1,)), ((), ())), precision=HIGHEST, preferred_element_type=F32
    )


def lower_kernel(out):
    out[...] = jnp.where(lower_mask(), 1.0, 0.0)


def position():
    index = lax.axis_index("ctx")
    return index & (NZ - 1), (index >> 3) & (NY - 1), index >> 5, lax.axis_index("tp")


def rows_of(index):
    return pl.ds(pl.multiple_of(index * W, W), W)


def local_state_kernel(group, lower, x, b, log_decay, keep, send, cum_ref):
    pos = position()
    cum_ref[...] = running_sum(log_decay[...], lower[...])
    b_t = b[...].astype(F32).T
    role = pos[0] & 1
    for out, side in ((send, 1 - role), (keep, role)):
        lasts = []
        for j in range(HALF):
            head = (group * 2 + side) * HALF + j
            cum = cum_ref[pl.ds(head, 1), :]
            last = jnp.broadcast_to(cum[:, W - 1 :], (1, W))
            parts = jnp.concatenate(split(b_t * jnp.exp(last - cum)), axis=1)
            x_head = x[:, rows_of(head)]
            out[j * W : (j + 1) * W, :] = jnp.dot(
                parts, jnp.concatenate([x_head, x_head]), preferred_element_type=F32
            )
            lasts.append(last)
        out[ROWS:, :] = decay_tile(lasts)


def pair_kernel(keep, got, *outs):
    pos = position()
    first = pos[0] & 1 == 0
    for k, m in enumerate(UP):
        j = (pos[0] >> 1) ^ m
        state, log = rows_of(j), pl.ds(ROWS + j, 1)
        earlier = jnp.where(first, keep[state, :], got[state, :])
        later = jnp.where(first, got[state, :], keep[state, :])
        decay = jnp.exp(jnp.where(first, got[log, :], keep[log, :]))
        outs[k][:W, :] = decay * earlier + later
        outs[k][W:, :] = decay_tile([keep[log, :] + got[log, :]])


def row_total_kernel(*refs):
    pos = position()
    parts, out = refs[:PAIRS], refs[PAIRS]
    places = [(pos[0] >> 1) ^ m for m in UP]
    logs = [part[W : W + 1, :] for part in parts]
    total = jnp.zeros((W, W), F32)
    for k in range(PAIRS):
        after = jnp.zeros((1, W), F32)
        for j in range(PAIRS):
            if j != k:
                after += jnp.where(places[j] > places[k], logs[j], 0.0)
        total += jnp.exp(after) * parts[k][:W, :]
    out[:W, :] = total
    out[W:, :] = decay_tile([sum(logs)])


def plane_kernel(*refs):
    pos = position()
    parts, plane, before = refs[:NY], refs[NY], refs[NY + 1]
    places = [pos[1] ^ m for m in ACROSS]
    logs = [part[W : W + 1, :] for part in parts]
    total = jnp.zeros((W, W), F32)
    earlier = jnp.zeros((W, W), F32)
    to_row = jnp.zeros((1, W), F32)
    for k in range(NY):
        after = jnp.zeros((1, W), F32)
        between = jnp.zeros((1, W), F32)
        for j in range(NY):
            if j != k:
                later = jnp.where(places[j] > places[k], logs[j], 0.0)
                after += later
                between += jnp.where(places[j] < pos[1], later, 0.0)
        piece = parts[k][:W, :]
        total += jnp.exp(after) * piece
        if k > 0:
            mine = places[k] < pos[1]
            earlier += jnp.where(mine, jnp.exp(between), 0.0) * piece
            to_row += jnp.where(mine, logs[k], 0.0)
    plane[:W, :] = total
    before[:W, :] = earlier
    plane[W:, :] = decay_tile([sum(logs)])
    before[W:, :] = decay_tile([to_row])


def entering_kernel(*refs):
    pos = position()
    planes, before = refs[: NX - 1], refs[NX - 1]
    parts = refs[NX : NX + PAIRS]
    outs = refs[NX + PAIRS : NX + 2 * PAIRS]
    ordered, entering = refs[NX + 2 * PAIRS :]
    for k, m in enumerate(UP):
        ordered[(pos[0] >> 1) ^ m] = parts[k][...]
    carry = jnp.zeros((W, W), F32)
    logs = [plane[W : W + 1, :] for plane in planes]
    places = [pos[2] ^ m for m in ACROSS[1:]]
    for k in range(NX - 1):
        after = jnp.zeros((1, W), F32)
        for j in range(NX - 1):
            if j != k:
                between = jnp.logical_and(places[j] > places[k], places[j] < pos[2])
                after += jnp.where(between, logs[j], 0.0)
        weight = jnp.where(places[k] < pos[2], jnp.exp(after), 0.0)
        carry += weight * planes[k][:W, :]
    carry = jnp.exp(before[W : W + 1, :]) * carry + before[:W, :]
    for place in range(PAIRS):
        entering[place] = carry
        if place < PAIRS - 1:
            carry = jnp.exp(ordered[place, W : W + 1, :]) * carry + ordered[place, :W, :]
    for k, m in enumerate(DOWN):
        outs[k][...] = entering[(pos[0] >> 1) ^ m]


def spread_kernel(keep, got, *refs):
    pos = position()
    carries, mine, send = refs[:PAIRS], refs[PAIRS], refs[PAIRS + 1]
    first = pos[0] & 1 == 0
    for k, m in enumerate(DOWN):
        j = (pos[0] >> 1) ^ m
        state, log = rows_of(j), pl.ds(ROWS + j, 1)
        carry = carries[k][...]
        decay = jnp.exp(jnp.where(first, keep[log, :], got[log, :]))
        after = decay * carry + jnp.where(first, keep[state, :], got[state, :])
        mine[state, :] = jnp.where(first, carry, after)
        send[state, :] = jnp.where(first, after, carry)


def inside_kernel(skip, ones, x, z, b, c, log_decay, gain, fixed, slope, read, gain_out):
    read[...] = c[...]
    gain_out[...] = gain[...]
    lower = lower_mask()
    logs = log_decay[...]
    cum = running_sum(logs, ones[...])
    cum_t = running_sum_t(logs, ones[...])
    scores = lax.dot_general(c[...], b[...], (((1,), (1,)), ((), ())), preferred_element_type=F32)
    for head in range(HEADS):
        at = slice(head * W, (head + 1) * W)
        column = cum_t[:, head : head + 1]
        differ = column - cum[head : head + 1, :]
        within = jnp.where(lower, jnp.exp(jnp.where(lower, differ, 0.0)), 0.0)
        x_head = x[:, at]
        inner = jnp.dot((within * scores).astype(BF16), x_head, preferred_element_type=F32)
        gate = z[:, at].astype(F32)
        gate = gate / (1.0 + jnp.exp(-gate))
        fixed[:, at] = (inner + skip[head] * x_head.astype(F32)) * gate
        slope[:, at] = jnp.exp(column) * gate


def finish_kernel(group, sides, stage, *refs):
    pos = position()
    count = len(sides)
    states, refs = refs[:count], refs[count:]
    read, fixed, slope, gain, w = refs[:5]
    first_row = 0
    if stage == 0:
        total, w_next, normed, sem = refs[5:]
        fetch = pltpu.make_async_copy(w.at[w_next.shape[0] :, :], w_next, sem)
        fetch.start()
    elif stage == 1:
        so_far, total, normed = refs[5:]
        first_row = w.shape[0]
    else:
        so_far, mine, other, normed, tile = refs[5:]
        left = w.shape[1] // 2
        first_row = w.shape[0]
    role = pos[0] & 1
    bases = [(group * 2 + (1 - role if side else role)) * HALF for side in sides]
    twice = jnp.concatenate([read[...], read[...]], axis=1)
    for k, base in enumerate(bases):
        for i in range(0, HALF, 2):
            parts = [split(states[k][(i + n) * W : (i + n + 1) * W, :]) for n in range(2)]
            both = [jnp.concatenate(half, axis=1) for half in zip(*parts)]
            carried = jnp.dot(twice, jnp.concatenate(both), preferred_element_type=F32)
            for n in range(2):
                head = base + i + n
                at = rows_of(head)
                gated = fixed[:, at] + slope[:, at] * carried[:, n * W : (n + 1) * W]
                meansq = jnp.mean(gated * gated, axis=-1, keepdims=True)
                value = gated * lax.rsqrt(meansq + 1e-05) * gain[pl.ds(head, 1), :]
                place = k * ROWS + (i + n) * W
                normed[:, place : place + W] = value.astype(BF16)
    for at in range(0, w.shape[1] if stage < 2 else left, TILE):
        columns = slice(at, at + TILE)
        part = jnp.zeros((W, TILE), F32) if stage == 0 else so_far[:, columns]
        for k, base in enumerate(bases):
            rows = pl.ds(pl.multiple_of(base * W - first_row, ROWS), ROWS)
            part += jnp.dot(
                normed[:, k * ROWS : (k + 1) * ROWS], w[rows, columns], preferred_element_type=F32
            )
        if stage < 2:
            total[:, columns] = part
        else:
            half = W // 2
            tile[...] = part
            mine[:, columns] = tile[pl.ds(pl.multiple_of(pos[3] * half, half), half), :]
            other[:, columns] = tile[pl.ds(pl.multiple_of((1 - pos[3]) * half, half), half), :]
    if stage == 0:
        fetch.wait()


def right_kernel(normed, w, so_far, mine, other, tile):
    pos = position()
    half, left = W // 2, mine.shape[1]
    rows = pl.ds(pl.multiple_of((1 - (pos[0] & 1)) * ROWS, ROWS), ROWS)
    for at in range(0, left, TILE):
        columns, source = slice(at, at + TILE), slice(left + at, left + at + TILE)
        tile[...] = so_far[:, source] + jnp.dot(
            normed[...], w[rows, source], preferred_element_type=F32
        )
        mine[:, columns] = tile[pl.ds(pl.multiple_of(pos[3] * half, half), half), :]
        other[:, columns] = tile[pl.ds(pl.multiple_of((1 - pos[3]) * half, half), half), :]


def add_kernel(near_left, near_right, left, right, out):
    middle = out.shape[1] // 2
    out[:, :middle] = (near_left[...] + left[...]).astype(BF16)
    out[:, middle:] = (near_right[...] + right[...]).astype(BF16)


def call(kernel, outs, specs, scratch=(), name=None, grant=16, work=0):
    return pl.pallas_call(
        kernel,
        out_shape=outs,
        in_specs=specs,
        out_specs=jax.tree.map(lambda _: VMEM, outs),
        scratch_shapes=scratch,
        compiler_params=pltpu.CompilerParams(vmem_limit_bytes=grant * 1024 * 1024),
        cost_estimate=pl.CostEstimate(flops=work, bytes_accessed=0, transcendentals=0),
        name=name,
    )


def shaped(*shape, dtype=F32):
    return jax.ShapeDtypeStruct(shape, dtype)


def exchange(values, stride, order):
    return [values[0]] + [
        lax.ppermute(value, "ctx", partners(stride, m)) for value, m in zip(values[1:], order[1:])
    ]


def per_device(x_in, z_in, b_in, c_in, log_decay, d_skip, norm_gain, w_out):
    lower = call(lower_kernel, shaped(W, W), [], name="lower", work=WORK)()
    lower, x_in, z_in, b_in, c_in, log_decay, d_skip, norm_gain = lax.optimization_barrier(
        (lower, x_in, z_in, b_in, c_in, log_decay, d_skip, norm_gain)
    )
    x = x_in.reshape(W, HEADS * W)
    width = w_out.shape[1]
    full, single = shaped(ROWS + 8, W), shaped(W + 8, W)
    keep, got, parts, totals, planes, mine, states = {}, {}, {}, {}, {}, {}, {}
    for g in range(GROUPS):
        keep[g], send = call(
            functools.partial(local_state_kernel, g), [full] * 2, [VMEM] * 4,
            [pltpu.VMEM((HEADS, W), F32)], name=f"local_state_{g}",
        )(lower, x, b_in, log_decay)
        got[g] = lax.ppermute(send, "ctx", partners(1, 1))
    keep[1], z = lax.optimization_barrier((keep[1], z_in))
    fixed, slope, read, gain = call(
        inside_kernel,
        [shaped(W, HEADS * W), shaped(W, HEADS * W), shaped(W, W, dtype=BF16), shaped(HEADS, W)],
        [SMEM] + [VMEM] * 7, name="inside",
    )(d_skip, lower, x, z.reshape(W, HEADS * W), b_in, c_in, log_decay, norm_gain)
    keep[0], fixed, slope, read, gain = lax.optimization_barrier(
        (keep[0], fixed, slope, read, gain)
    )
    for g in range(GROUPS):
        pair = call(pair_kernel, [single] * PAIRS, [VMEM] * 2, name=f"pair_{g}")(
            keep[g], got[g]
        )
        parts[g] = exchange(pair, 2, UP)
    for g in range(GROUPS):
        total = call(
            row_total_kernel, single, [VMEM] * PAIRS, name=f"row_total_{g}"
        )(*parts[g])
        totals[g] = exchange([total] * NY, NZ, ACROSS)
    for g in range(GROUPS):
        plane, before = call(
            plane_kernel, [single] * 2, [VMEM] * NY, name=f"plane_{g}"
        )(*totals[g])
        planes[g] = exchange([plane] * NX, NY * NZ, ACROSS)[1:] + [before]
    for g in range(GROUPS):
        back = call(
            entering_kernel, [shaped(W, W)] * PAIRS, [VMEM] * (NX + PAIRS),
            [pltpu.VMEM((PAIRS, W + 8, W), F32), pltpu.VMEM((PAIRS, W, W), F32)],
            name=f"entering_{g}", work=WORK,
        )(*planes[g], *parts[g])
        states[g] = exchange(back, 2, DOWN)
    for g in range(GROUPS):
        mine[g], send = call(
            spread_kernel, [shaped(ROWS, W)] * 2, [VMEM] * (2 + PAIRS), name=f"spread_{g}"
        )(keep[g], got[g], *states[g])
        states[g] = lax.ppermute(send, "ctx", partners(1, 1))

    def finish(group, sides, stage, parts, w, outs, extra):
        scratch = [pltpu.VMEM((W, len(sides) * ROWS), BF16)] if stage < 2 else []
        scratch += [[pltpu.SemaphoreType.DMA(())], [], [pltpu.VMEM((W, TILE), F32)]][stage]
        return call(
            functools.partial(finish_kernel, group, sides, stage), outs,
            [VMEM] * (len(sides) + 5 + len(extra)), scratch, name=f"finish_{stage}",
        )(*parts, read, fixed, slope, gain, w, *extra)

    so_far, w = finish(
        0, (0, 1), 0, [mine[0], states[0]], w_out,
        [shaped(W, width), shaped(w_out.shape[0] // 2, width, dtype=BF16)], [],
    )
    so_far = finish(1, (0,), 1, [mine[1]], w, shaped(W, width), [so_far])
    quarter = shaped(W // 2, width // 2)
    swap = [(0, 1), (1, 0)]
    near_left, far_left, normed = finish(
        1, (1,), 2, [states[1]], w, [quarter, quarter, shaped(W, ROWS, dtype=BF16)], [so_far]
    )
    left = lax.ppermute(far_left, "tp", swap)
    near_right, far_right = call(
        right_kernel, [quarter] * 2, [VMEM] * 3, [pltpu.VMEM((W, TILE), F32)], name="finish_right"
    )(normed, w, so_far)
    right = lax.ppermute(far_right, "tp", swap)
    return call(add_kernel, shaped(W // 2, width, dtype=BF16), [VMEM] * 4, name="add")(
        near_left, near_right, left, right
    )


def solution(mesh):
    return jax.shard_map(
        per_device,
        mesh=mesh,
        in_specs=(
            P("ctx", "tp", None),
            P("ctx", "tp", None),
            P("ctx", None),
            P("ctx", None),
            P("tp", "ctx"),
            P("tp"),
            P("tp", None),
            P("tp", None),
        ),
        out_specs=P(("ctx", "tp"), None),
        check_vma=False,
    )
```

```python
import functools

import jax
import jax.numpy as jnp
from jax import lax
from jax.experimental import pallas as pl
from jax.experimental.pallas import tpu as pltpu
from jax.sharding import PartitionSpec as P

F32 = jnp.float32
BF16 = jnp.bfloat16
HIGHEST = lax.Precision.HIGHEST
NX, NY, NZ = 4, 4, 8
PAIRS = NZ // 2
HEADS = 16
W = 128
GROUPS = 2
HALF = HEADS // GROUPS // 2
ROWS = HALF * W
TILE = 512
WORK = 10**10
UP = ((0, 3, 2, 1), (0, 3, 2, 1))
DOWN = ((0, 1, 2, 3), (0, 3, 2, 1))
ACROSS = (0, 1, 2, 3)
VMEM = pl.BlockSpec(memory_space=pltpu.VMEM)
SMEM = pl.BlockSpec(memory_space=pltpu.SMEM)


def partners(stride, k):
    return [(i, i ^ (stride * k)) for i in range(NX * NY * NZ)]


def split(value):
    high = value.astype(BF16)
    return high, (value - high.astype(F32)).astype(BF16)


def lower_mask():
    rows = lax.broadcasted_iota(jnp.int32, (W, W), 0)
    columns = lax.broadcasted_iota(jnp.int32, (W, W), 1)
    return rows >= columns


def running_sum(log_decay, lower):
    return lax.dot_general(
        log_decay, lower, (((1,), (1,)), ((), ())), precision=HIGHEST, preferred_element_type=F32
    )


def decay_tile(rows):
    place = lax.broadcasted_iota(jnp.int32, (8, W), 0)
    tile = jnp.zeros((8, W), F32)
    for i, row in enumerate(rows):
        tile = jnp.where(place == i, jnp.broadcast_to(row, (8, W)), tile)
    return tile


def running_sum_t(log_decay, lower):
    return lax.dot_general(
        lower, log_decay, (((1,), (1,)), ((), ())), precision=HIGHEST, preferred_element_type=F32
    )


def lower_kernel(out):
    out[...] = jnp.where(lower_mask(), 1.0, 0.0)


def position():
    index = lax.axis_index("ctx")
    return index & (NZ - 1), (index >> 3) & (NY - 1), index >> 5, lax.axis_index("tp")


def rows_of(index):
    return pl.ds(pl.multiple_of(index * W, W), W)


def local_state_kernel(group, lower, x, b, log_decay, keep, send, cum_ref):
    pos = position()
    cum_ref[...] = running_sum(log_decay[...], lower[...])
    b_t = b[...].astype(F32).T
    role = pos[0] & 1
    for out, side in ((send, 1 - role), (keep, role)):
        lasts = []
        for j in range(HALF):
            head = (group * 2 + side) * HALF + j
            cum = cum_ref[pl.ds(head, 1), :]
            last = jnp.broadcast_to(cum[:, W - 1 :], (1, W))
            parts = jnp.concatenate(split(b_t * jnp.exp(last - cum)), axis=1)
            x_head = x[:, rows_of(head)]
            out[j * W : (j + 1) * W, :] = jnp.dot(
                parts, jnp.concatenate([x_head, x_head]), preferred_element_type=F32
            )
            lasts.append(last)
        out[ROWS:, :] = decay_tile(lasts)


def pair_kernel(group, keep, got, *outs):
    pos = position()
    first = pos[0] & 1 == 0
    for k, m in enumerate(UP[group]):
        j = (pos[0] >> 1) ^ m
        state, log = rows_of(j), pl.ds(ROWS + j, 1)
        earlier = jnp.where(first, keep[state, :], got[state, :])
        later = jnp.where(first, got[state, :], keep[state, :])
        decay = jnp.exp(jnp.where(first, got[log, :], keep[log, :]))
        outs[k][:W, :] = decay * earlier + later
        outs[k][W:, :] = decay_tile([keep[log, :] + got[log, :]])


def row_total_kernel(group, *refs):
    pos = position()
    parts, out = refs[:PAIRS], refs[PAIRS]
    places = [(pos[0] >> 1) ^ m for m in UP[group]]
    logs = [part[W : W + 1, :] for part in parts]
    total = jnp.zeros((W, W), F32)
    for k in range(PAIRS):
        after = jnp.zeros((1, W), F32)
        for j in range(PAIRS):
            if j != k:
                after += jnp.where(places[j] > places[k], logs[j], 0.0)
        total += jnp.exp(after) * parts[k][:W, :]
    out[:W, :] = total
    out[W:, :] = decay_tile([sum(logs)])


def plane_kernel(*refs):
    pos = position()
    parts, plane, before = refs[:NY], refs[NY], refs[NY + 1]
    places = [pos[1] ^ m for m in ACROSS]
    logs = [part[W : W + 1, :] for part in parts]
    total = jnp.zeros((W, W), F32)
    earlier = jnp.zeros((W, W), F32)
    to_row = jnp.zeros((1, W), F32)
    for k in range(NY):
        after = jnp.zeros((1, W), F32)
        between = jnp.zeros((1, W), F32)
        for j in range(NY):
            if j != k:
                later = jnp.where(places[j] > places[k], logs[j], 0.0)
                after += later
                between += jnp.where(places[j] < pos[1], later, 0.0)
        piece = parts[k][:W, :]
        total += jnp.exp(after) * piece
        if k > 0:
            mine = places[k] < pos[1]
            earlier += jnp.where(mine, jnp.exp(between), 0.0) * piece
            to_row += jnp.where(mine, logs[k], 0.0)
    plane[:W, :] = total
    before[:W, :] = earlier
    plane[W:, :] = decay_tile([sum(logs)])
    before[W:, :] = decay_tile([to_row])


def entering_kernel(group, *refs):
    pos = position()
    planes, before = refs[: NX - 1], refs[NX - 1]
    parts = refs[NX : NX + PAIRS]
    outs = refs[NX + PAIRS : NX + 2 * PAIRS]
    ordered, entering = refs[NX + 2 * PAIRS :]
    for k, m in enumerate(UP[group]):
        ordered[(pos[0] >> 1) ^ m] = parts[k][...]
    carry = jnp.zeros((W, W), F32)
    logs = [plane[W : W + 1, :] for plane in planes]
    places = [pos[2] ^ m for m in ACROSS[1:]]
    for k in range(NX - 1):
        after = jnp.zeros((1, W), F32)
        for j in range(NX - 1):
            if j != k:
                between = jnp.logical_and(places[j] > places[k], places[j] < pos[2])
                after += jnp.where(between, logs[j], 0.0)
        weight = jnp.where(places[k] < pos[2], jnp.exp(after), 0.0)
        carry += weight * planes[k][:W, :]
    carry = jnp.exp(before[W : W + 1, :]) * carry + before[:W, :]
    for place in range(PAIRS):
        entering[place] = carry
        if place < PAIRS - 1:
            carry = jnp.exp(ordered[place, W : W + 1, :]) * carry + ordered[place, :W, :]
    for k, m in enumerate(DOWN[group]):
        outs[k][...] = entering[(pos[0] >> 1) ^ m]


def spread_kernel(group, keep, got, *refs):
    pos = position()
    carries, mine, send = refs[:PAIRS], refs[PAIRS], refs[PAIRS + 1]
    first = pos[0] & 1 == 0
    for k, m in enumerate(DOWN[group]):
        j = (pos[0] >> 1) ^ m
        state, log = rows_of(j), pl.ds(ROWS + j, 1)
        carry = carries[k][...]
        decay = jnp.exp(jnp.where(first, keep[log, :], got[log, :]))
        after = decay * carry + jnp.where(first, keep[state, :], got[state, :])
        mine[state, :] = jnp.where(first, carry, after)
        send[state, :] = jnp.where(first, after, carry)


def inside_kernel(skip, ones, x, z, b, c, log_decay, gain, fixed, slope, read, gain_out):
    read[...] = c[...]
    gain_out[...] = gain[...]
    lower = lower_mask()
    logs = log_decay[...]
    cum = running_sum(logs, ones[...])
    cum_t = running_sum_t(logs, ones[...])
    scores = lax.dot_general(c[...], b[...], (((1,), (1,)), ((), ())), preferred_element_type=F32)
    for head in range(HEADS):
        at = slice(head * W, (head + 1) * W)
        column = cum_t[:, head : head + 1]
        differ = column - cum[head : head + 1, :]
        within = jnp.where(lower, jnp.exp(jnp.where(lower, differ, 0.0)), 0.0)
        x_head = x[:, at]
        inner = jnp.dot((within * scores).astype(BF16), x_head, preferred_element_type=F32)
        gate = z[:, at].astype(F32)
        gate = gate / (1.0 + jnp.exp(-gate))
        fixed[:, at] = (inner + skip[head] * x_head.astype(F32)) * gate
        slope[:, at] = jnp.exp(column) * gate


def finish_kernel(group, sides, stage, *refs):
    pos = position()
    count = len(sides)
    states, refs = refs[:count], refs[count:]
    read, fixed, slope, gain, w = refs[:5]
    first_row = 0
    if stage == 0:
        total, w_next, normed, sem = refs[5:]
        fetch = pltpu.make_async_copy(w.at[w_next.shape[0] :, :], w_next, sem)
        fetch.start()
    elif stage == 1:
        so_far, total, normed = refs[5:]
        first_row = w.shape[0]
    else:
        so_far, mine, other, normed, tile = refs[5:]
        first_row = w.shape[0]
    role = pos[0] & 1
    bases = [(group * 2 + (1 - role if side else role)) * HALF for side in sides]
    twice = jnp.concatenate([read[...], read[...]], axis=1)
    for k, base in enumerate(bases):
        for i in range(0, HALF, 2):
            parts = [split(states[k][(i + n) * W : (i + n + 1) * W, :]) for n in range(2)]
            both = [jnp.concatenate(half, axis=1) for half in zip(*parts)]
            carried = jnp.dot(twice, jnp.concatenate(both), preferred_element_type=F32)
            for n in range(2):
                head = base + i + n
                at = rows_of(head)
                gated = fixed[:, at] + slope[:, at] * carried[:, n * W : (n + 1) * W]
                meansq = jnp.mean(gated * gated, axis=-1, keepdims=True)
                value = gated * lax.rsqrt(meansq + 1e-05) * gain[pl.ds(head, 1), :]
                place = k * ROWS + (i + n) * W
                normed[:, place : place + W] = value.astype(BF16)
    for at in range(0, w.shape[1], TILE):
        columns = slice(at, at + TILE)
        part = jnp.zeros((W, TILE), F32) if stage == 0 else so_far[:, columns]
        for k, base in enumerate(bases):
            rows = pl.ds(pl.multiple_of(base * W - first_row, ROWS), ROWS)
            part += jnp.dot(
                normed[:, k * ROWS : (k + 1) * ROWS], w[rows, columns], preferred_element_type=F32
            )
        if stage < 2:
            total[:, columns] = part
        else:
            half = W // 2
            tile[...] = part
            mine[:, columns] = tile[pl.ds(pl.multiple_of(pos[3] * half, half), half), :]
            other[:, columns] = tile[pl.ds(pl.multiple_of((1 - pos[3]) * half, half), half), :]
    if stage == 0:
        fetch.wait()


def call(kernel, outs, specs, scratch=(), name=None, grant=16, work=0):
    return pl.pallas_call(
        kernel,
        out_shape=outs,
        in_specs=specs,
        out_specs=jax.tree.map(lambda _: VMEM, outs),
        scratch_shapes=scratch,
        compiler_params=pltpu.CompilerParams(vmem_limit_bytes=grant * 1024 * 1024),
        cost_estimate=pl.CostEstimate(flops=work, bytes_accessed=0, transcendentals=0),
        name=name,
    )


def shaped(*shape, dtype=F32):
    return jax.ShapeDtypeStruct(shape, dtype)


def exchange(values, stride, order):
    return [values[0]] + [
        lax.ppermute(value, "ctx", partners(stride, m)) for value, m in zip(values[1:], order[1:])
    ]


def per_device(x_in, z_in, b_in, c_in, log_decay, d_skip, norm_gain, w_out):
    lower = call(lower_kernel, shaped(W, W), [], name="lower", work=WORK)()
    lower, x_in, z_in, b_in, c_in, log_decay, d_skip, norm_gain = lax.optimization_barrier(
        (lower, x_in, z_in, b_in, c_in, log_decay, d_skip, norm_gain)
    )
    x = x_in.reshape(W, HEADS * W)
    width = w_out.shape[1]
    full, single = shaped(ROWS + 8, W), shaped(W + 8, W)
    keep, got, parts, totals, planes, mine, states = {}, {}, {}, {}, {}, {}, {}
    for g in range(GROUPS):
        keep[g], send = call(
            functools.partial(local_state_kernel, g), [full] * 2, [VMEM] * 4,
            [pltpu.VMEM((HEADS, W), F32)], name=f"local_state_{g}",
        )(lower, x, b_in, log_decay)
        got[g] = lax.ppermute(send, "ctx", partners(1, 1))
    keep[1], z = lax.optimization_barrier((keep[1], z_in))
    fixed, slope, read, gain = call(
        inside_kernel,
        [shaped(W, HEADS * W), shaped(W, HEADS * W), shaped(W, W, dtype=BF16), shaped(HEADS, W)],
        [SMEM] + [VMEM] * 7, name="inside",
    )(d_skip, lower, x, z.reshape(W, HEADS * W), b_in, c_in, log_decay, norm_gain)
    keep[0], fixed, slope, read, gain = lax.optimization_barrier(
        (keep[0], fixed, slope, read, gain)
    )
    for g in range(GROUPS):
        pair = call(functools.partial(pair_kernel, g), [single] * PAIRS, [VMEM] * 2, name=f"pair_{g}")(
            keep[g], got[g]
        )
        parts[g] = exchange(pair, 2, UP[g])
    for g in range(GROUPS):
        total = call(
            functools.partial(row_total_kernel, g), single, [VMEM] * PAIRS, name=f"row_total_{g}"
        )(*parts[g])
        totals[g] = exchange([total] * NY, NZ, ACROSS)
    for g in range(GROUPS):
        plane, before = call(
            plane_kernel, [single] * 2, [VMEM] * NY, name=f"plane_{g}"
        )(*totals[g])
        planes[g] = exchange([plane] * NX, NY * NZ, ACROSS)[1:] + [before]
    for g in range(GROUPS):
        back = call(
            functools.partial(entering_kernel, g), [shaped(W, W)] * PAIRS, [VMEM] * (NX + PAIRS),
            [pltpu.VMEM((PAIRS, W + 8, W), F32), pltpu.VMEM((PAIRS, W, W), F32)],
            name=f"entering_{g}", work=WORK,
        )(*planes[g], *parts[g])
        states[g] = exchange(back, 2, DOWN[g])
    for g in range(GROUPS):
        mine[g], send = call(
            functools.partial(spread_kernel, g), [shaped(ROWS, W)] * 2, [VMEM] * (2 + PAIRS), name=f"spread_{g}"
        )(keep[g], got[g], *states[g])
        states[g] = lax.ppermute(send, "ctx", partners(1, 1))

    def finish(group, sides, stage, parts, w, outs, extra):
        scratch = [pltpu.VMEM((W, len(sides) * ROWS), BF16)]
        scratch += [[pltpu.SemaphoreType.DMA(())], [], [pltpu.VMEM((W, TILE), F32)]][stage]
        return call(
            functools.partial(finish_kernel, group, sides, stage), outs,
            [VMEM] * (len(sides) + 5 + len(extra)), scratch, name=f"finish_{stage}",
        )(*parts, read, fixed, slope, gain, w, *extra)

    so_far, w = finish(
        0, (0, 1), 0, [mine[0], states[0]], w_out,
        [shaped(W, width), shaped(w_out.shape[0] // 2, width, dtype=BF16)], [],
    )
    so_far = finish(1, (0,), 1, [mine[1]], w, shaped(W, width), [so_far])
    near, far = finish(1, (1,), 2, [states[1]], w, [shaped(W // 2, width)] * 2, [so_far])
    return (near + lax.ppermute(far, "tp", [(0, 1), (1, 0)])).astype(BF16)


def solution(mesh):
    return jax.shard_map(
        per_device,
        mesh=mesh,
        in_specs=(
            P("ctx", "tp", None),
            P("ctx", "tp", None),
            P("ctx", None),
            P("ctx", None),
            P("tp", "ctx"),
            P("tp"),
            P("tp", None),
            P("tp", None),
        ),
        out_specs=P(("ctx", "tp"), None),
        check_vma=False,
    )
```
